512 devices in a mesh: row: 64 (over x, y, core), col: 8 (over z).
Axes of the slice: x: 4, y: 8, z: 8, core: 2. Of those that a mesh axis runs over, the one named last changes fastest.
Arguments:
- pivot: float32 [1024, 1024], P('row')
- panel: bfloat16 [65536, 1024], P('row', 'col'), may hold values from -6 to 6
- slab: bfloat16 [65536, 2048], P('row', 'col'), may hold values from -6 to 6
- pattern: int32 [512, 16], P('row', 'col'), may hold values 0 or 1
- col_source: int32 [16], P('col'), may hold values from 0 to 511, as said below
Outputs:
- factor_panel: bfloat16 [65536, 1024], P('row', 'col')
- updated_slab: bfloat16 [65536, 2048], P('row', 'col')
The draws below stay inside these ranges and needn't reach their ends.
Inputs may be any that keep to these rules, and one draw needn't show every extreme that they name: `col_source`: distinct block rows; block rows 0 and 511 are always among them.
All inputs are finite; a program needn't handle non-finite values. No bound on the sum of `pattern` on one device may be relied on, other than what follows from the above.
Results may differ from the reference program's by a relative error of at most 0.015.
Values may be sent and summed in bfloat16 or wider, within the bound.
A program may use at most 64 MiB of HBM per device.

```python
import jax
import jax.numpy as jnp
from jax import lax

BLOCK = 128
ROW_BLOCKS = 8
WIDE = 1024
TR = 512
TC = 16
N_ROW = 64


def kernel_pivot(key_points, key_diag, key_scale, reach, diag_lo, diag_hi, scale_lo, scale_hi):
    points = jax.random.uniform(key_points, (3, WIDE), jnp.float32, 0.0, 1.0)
    gaps = points[:, :, None] - points[:, None, :]
    distance = jnp.sqrt(jnp.sum(gaps * gaps, axis=0))
    kernel = jnp.exp(-distance / reach)
    scales = jax.random.uniform(key_scale, (WIDE,), jnp.float32, scale_lo, scale_hi)
    extra_diag = jax.random.uniform(key_diag, (WIDE,), jnp.float32, diag_lo, diag_hi)
    identity = jnp.eye(WIDE, dtype=jnp.float32)
    return kernel * scales[:, None] * scales[None, :] + identity * extra_diag[None, :]


def draw_pivot(key, part):
    key = jax.random.fold_in(key, 11)
    key_points, key_diag, key_scale = jax.random.split(key, 3)
    result = kernel_pivot(key_points, key_diag, key_scale, 0.15, 2.0, 20.0, 0.6, 1.4)
    return result


def draw_col_source(key, part):
    key = jax.random.fold_in(key, 23)
    key_pick, key_order = jax.random.split(key, 2)
    middle = jax.random.permutation(key_pick, TR - 2)[:TC - 2].astype(jnp.int32) + 1
    ends = jnp.array([0, TR - 1], dtype=jnp.int32)
    chosen = jnp.concatenate([ends, middle])
    order = jax.random.permutation(key_order, TC)
    return chosen[order].astype(jnp.int32)


def place_ends(values, stream_key, low, top_value):
    index_at = [jax.random.randint(jax.random.fold_in(stream_key, axis), (), 0, length) for axis, length in enumerate(values.shape)]
    widest = values.shape.index(max(values.shape))
    next_to = index_at[:widest] + [(index_at[widest] + 1) % values.shape[widest]] + index_at[widest + 1:]
    return values.at[tuple(index_at)].set(low).at[tuple(next_to)].set(top_value)


def block_scale(own_key, dims, cuts, low, high):
    gain = 1.0
    for dim, blocks in cuts:
        steps = jax.random.uniform(jax.random.fold_in(jax.random.fold_in(own_key, 6), dim), (blocks,), jnp.float32, low / len(cuts), high / len(cuts))
        gain = gain * jnp.repeat(jnp.exp(steps), dims[dim] // blocks).reshape((-1,) + (1,) * (len(dims) - 1 - dim))
    return gain


def scatter_about(stream_key, dims, scale, limit, pieces=(), kind=jnp.bfloat16):
    level = block_scale(stream_key, dims, pieces, -0.22, 0.18) if pieces else 1.0
    values = jax.random.normal(stream_key, dims, jnp.float32) * scale * level
    return jnp.minimum(jnp.maximum(values, -limit), limit).astype(kind)


def setup_inputs(seed: int = 0) -> dict:
    seeds = jax.random.split(jax.random.key(seed), 6)
    return {
        "pivot": draw_pivot(jax.random.fold_in(seeds[5], 71), 0),
        "panel": scatter_about(seeds[1], (TR * BLOCK, WIDE), 1.0, 6.0, ((0, 64), (1, 8))),
        "slab": scatter_about(seeds[2], (TR * BLOCK, TC * BLOCK), 1.0, 6.0, ((0, 64), (1, 8))),
        "pattern": place_ends((jax.random.randint(seeds[3], (TR, TC), 0, 2) < 1).astype(jnp.int32), jax.random.fold_in(seeds[3], 1), 0, 1),
        "col_source": draw_col_source(jax.random.fold_in(seeds[5], 71), 0),
    }


def reference(pivot, panel, slab, pattern, col_source):
    pivot_factor = jnp.linalg.cholesky(pivot)
    solved = jax.scipy.linalg.solve_triangular(pivot_factor, panel.astype(jnp.float32).T, lower=True).T
    factor_panel = solved.astype(jnp.bfloat16)
    wide_total = factor_panel.shape[1]
    blocked = factor_panel.reshape(TR, BLOCK, wide_total)
    picked = jnp.take(blocked, col_source.astype(jnp.int32), axis=0).reshape(TC * BLOCK, wide_total)
    row_groups = factor_panel.reshape(N_ROW, ROW_BLOCKS * BLOCK, wide_total)
    slab_groups = slab.reshape(N_ROW, ROW_BLOCKS * BLOCK, TC * BLOCK)
    mask_groups = pattern.reshape(N_ROW, ROW_BLOCKS, TC)

    def one_group(group_items):
        rows_here, slab_here, mask_here = group_items
        update = jnp.dot(rows_here.astype(jnp.float32), picked.T.astype(jnp.float32), preferred_element_type=jnp.float32)
        widened = jnp.repeat(jnp.repeat(mask_here.astype(jnp.float32), BLOCK, axis=0), BLOCK, axis=1)
        return (widened * (slab_here.astype(jnp.float32) - update)).astype(jnp.bfloat16)
    updated = lax.map(one_group, (row_groups, slab_groups, mask_groups))
    return (factor_panel, updated.reshape(TR * BLOCK, TC * BLOCK))
```

```python
import jax
import jax.numpy as jnp
from jax import lax
from jax.experimental import pallas as pl
from jax.experimental.pallas import tpu as pltpu
from jax.sharding import PartitionSpec as P

F32, BF16, I32 = jnp.float32, jnp.bfloat16, jnp.int32
B = 128
NB = 8
N = 1024
MESH = pl.DeviceIdType.MESH
GROUPS = ((0, 1), (1, 2), (2, 4), (4, 8))
NT = (((1,), (1,)), ((), ()))
NN = (((1,), (0,)), ((), ()))


def dot(a, b, dims=NT):
    return lax.dot_general(a, b, dims, preferred_element_type=F32)


def lane_spread(x, lane):
    return jnp.broadcast_to(x[:, lane : lane + 1], (8, B))


def row_spread(x, row):
    return jnp.broadcast_to(x[row : row + 1, :], (8, B))


def factor(rows, w_ref, aside):
    lane = lax.broadcasted_iota(I32, (8, B), 1)
    sub = lax.broadcasted_iota(I32, (8, B), 0)
    rows = list(rows)
    before = None
    for p in range(16):
        cols = [lane_spread(rows[p], 8 * p + j) for j in range(8)]
        inside = (lane >= 8 * p) & (lane < 8 * p + 8)
        unit = jnp.where(lane == 8 * p + sub, 1.0, 0.0).astype(F32)
        low = jnp.where(inside, unit, rows[p])
        full = low
        inverse = jnp.zeros((8, B), F32)
        for k in range(8):
            inv = 1.0 / row_spread(cols[k], k)
            mult = cols[k] * inv
            both = jnp.where(sub == k, 0.0, mult)
            below = jnp.where(sub > k, mult, 0.0)
            full = full - both * row_spread(full, k)
            low = low - below * row_spread(low, k)
            inverse = jnp.where(sub == k, inv, inverse)
            for j in range(k + 1, 8):
                cols[j] = cols[j] - both * row_spread(cols[j], k)
        w = jnp.where(lane < 8 * p + 8, low * jnp.sqrt(inverse), 0.0)
        if p % 2 == 0:
            before = w
        else:
            w_ref[8 * p - 8 : 8 * p + 8, :] = jnp.concatenate([before, w], 0).astype(BF16)
        full = full * inverse
        spread = [row_spread(full, k) for k in range(8)]
        for q in range(p + 1, 16):
            v = rows[q]
            t = [lane_spread(v, 8 * p + k) * spread[k] for k in range(8)]
            total = ((t[0] + t[1]) + (t[2] + t[3])) + ((t[4] + t[5]) + (t[6] + t[7]))
            rows[q] = jnp.where(inside, 0.0, v) - total
        aside(p)


def kernel(
    pivot, panel, slab, pattern, col_source, own_out, slab_out,
    piv, cs, marked, part1, part2, part3, pick, rows, lu, tcol, quad, w_ref, low_w, fac,
    y_send, y_recv, q_send, q_recv, c_send, c_recv, p_send, p_recv,
    s1_send, s1_recv, s2_send, s2_recv, s3_send, s3_recv, s4_send, s4_recv, s5_send, s5_recv,
):
    r = lax.axis_index("row")
    z = lax.axis_index("col")
    x, y, core = r // 16, (r // 2) % 8, r % 2
    q = x * 2 + core

    def at_y(d):
        return ((x * 8 + (y + d) % 8) * 2 + core, z)

    def at_q(d):
        o = (q + d) % 8
        return (((o // 2) * 8 + y) * 2 + o % 2, z)

    def at_z(d):
        return (r, (z + d) % 8)

    def remote(src, dst, send, recv, device):
        return pltpu.make_async_remote_copy(
            src_ref=src, dst_ref=dst, send_sem=send, recv_sem=recv,
            device_id=device, device_id_type=MESH,
        )

    def y_copy(g, d):
        a, b = GROUPS[g]
        ref = piv.at[a:b, x * 8 + y, core]
        return remote(ref, ref, y_send.at[g, d], y_recv.at[g, d], at_y(d))

    def q_copy(g, d):
        a, b = GROUPS[g]
        ref = piv.at[a:b, pl.ds(x * 8, 8), core]
        return remote(ref, ref, q_send.at[g, d], q_recv.at[g, d], at_q(d))

    def c_copy(d):
        ref = cs.at[z]
        return remote(ref, ref, c_send.at[d], c_recv.at[d], at_z(d))

    def p_copy(d):
        return remote(panel, rows.at[z], p_send.at[d], p_recv.at[d], at_z(d))

    def s1_copy(d):
        return remote(
            marked.at[(q + d) % 8], part1.at[d], s1_send.at[d], s1_recv.at[d], at_q(d)
        )

    def s2_copy(d):
        return remote(
            part2.at[0, pl.ds(((y + d) % 8) * 32, 32)], part2.at[d, 0:32],
            s2_send.at[d], s2_recv.at[d], at_y(d),
        )

    def s3_copy(source):
        return remote(
            part3.at[0], part3.at[1 + source], s3_send, s3_recv.at[source], (r, q)
        )

    def s4_copy(d):
        ref = pick.at[y]
        return remote(ref, ref, s4_send.at[d], s4_recv.at[d], at_q(d))

    def s5_copy(d):
        ref = pick.at[y]
        return remote(ref, ref, s5_send.at[d], s5_recv.at[d], at_y(d))

    others = range(1, 8)

    barrier = pltpu.get_barrier_semaphore()
    for d in others:
        for device in (at_y(d), at_q(d), at_z(d)):
            pl.semaphore_signal(barrier, inc=1, device_id=device, device_id_type=MESH)

    for c in range(NB):
        piv[c, x * 8 + y, core] = pivot[:, c * B : (c + 1) * B].astype(BF16)
    sub = lax.broadcasted_iota(I32, (8, B), 0)
    cs[z] = jnp.where(sub == 0, col_source[0], col_source[1])

    pl.semaphore_wait(barrier, 21)
    for d in others:
        y_copy(0, d).start()
    for d in others:
        c_copy(d).start()
    for g in (1, 2, 3):
        for d in others:
            y_copy(g, d).start()
    rows[z] = panel[...]
    lu[...] = jnp.zeros_like(lu)
    quad[...] = jnp.zeros_like(quad)
    tcol[...] = jnp.zeros_like(tcol)
    w_ref[...] = jnp.zeros_like(w_ref)
    for d in others:
        y_copy(0, d).wait_recv()
    for d in others:
        q_copy(0, d).start()

    for d in others:
        c_copy(d).wait_recv()

    def mark(pair, carry):
        for t in range(2):
            wanted = cs[pair, t : t + 1, :]
            total = jnp.zeros((B, B), F32)
            for s in range(8):
                here = panel[s * B : (s + 1) * B, :].astype(F32)
                total = jnp.where(wanted == r * 8 + s, here, total)
            marked[pair, t * B : (t + 1) * B, :] = total.astype(BF16)
        return carry

    lax.fori_loop(0, 8, mark, 0)
    for g in (1, 2):
        for d in others:
            y_copy(g, d).wait_recv()
        for d in others:
            q_copy(g, d).start()
    for d in others:
        s1_copy(d).start()
    for d in others:
        p_copy(d).start()
    for d in others:
        y_copy(3, d).wait_recv()
    for d in others:
        q_copy(3, d).start()

    def block_rows(column, block):
        return piv[column, pl.ds(block * 4, 4)].reshape(B, B)

    def arrive(j):
        for g, (a, _) in enumerate(GROUPS):
            @pl.when(j == a)
            def _():
                for d in others:
                    q_copy(g, d).wait_recv()

        @pl.when(j == 1)
        def _():
            total = marked[q].astype(F32)
            for d in others:
                s1_copy(d).wait_recv()
            for d in others:
                total += part1[d].astype(F32)
            part2[0] = total.astype(BF16)
            for d in others:
                s2_copy(d).start()

        @pl.when(j == 2)
        def _():
            for d in others:
                s2_copy(d).wait_recv()
            total = part2[0, pl.ds(y * 32, 32), :].astype(F32)
            for d in others:
                total += part2[d, 0:32, :].astype(F32)
            part3[0] = total.astype(BF16)

            @pl.when(z != q)
            def _():
                s3_copy(z).start()

        @pl.when((j == 3) & (z == q))
        def _():
            for s in range(8):
                @pl.when(z != s)
                def _():
                    s3_copy(s).wait_recv()
                    pick[y, s] = part3[1 + s]
            pick[y, z] = part3[0]
            for d in others:
                s4_copy(d).start()

        @pl.when(j == 4)
        def _():
            for d in others:
                @pl.when((q + 8 - d) % 8 == z)
                def _():
                    s4_copy(d).wait_recv()
            for d in others:
                s5_copy(d).start()

    def step(j, carry):
        arrive(j)
        jm = jnp.maximum(j - 1, 0)
        jn = jnp.minimum(j + 1, NB - 1)
        now = pl.ds(pl.multiple_of(j * B, B), B)
        last = pl.ds(pl.multiple_of(jm * B, B), B)
        after = pl.ds(pl.multiple_of(jn * B, B), B)
        w_old = w_ref[...]
        row_j = lu[0, now, :]
        diagonal = block_rows(j, j).astype(F32) - quad[...]
        eye = jnp.where(
            lax.broadcasted_iota(I32, (B, B), 0) == lax.broadcasted_iota(I32, (B, B), 1), 1.0, 0.0
        ).astype(F32)

        def aside(p):
            block, half = p // 2, p % 2
            part = slice(p * 64, (p + 1) * 64)
            was_below = jnp.where(block > jm, 0, 1)
            done = dot(tcol[part, :], w_old).astype(BF16)
            lu[was_below, part, last] = done
            upper = jnp.where(block > j, 0, 1)
            t = -dot(lu[upper, part, :], row_j)
            source = piv[j, block * 4 + half * 2 : block * 4 + half * 2 + 2].reshape(64, B)
            keep = jnp.where(block > j, 1.0, 0.0).astype(F32)
            on = jnp.where(block == j, 1.0, 0.0).astype(F32)
            t = t + source.astype(F32) * keep + eye[half * 64 : half * 64 + 64, :] * on
            tcol[part, :] = t.astype(BF16)

        factor([diagonal[8 * i : 8 * i + 8, :] for i in range(16)], w_ref, aside)
        row_next = lu[0, after, :]
        total = dot(row_next, row_next)
        new = dot(tcol[after, :], w_ref[...]).astype(BF16)
        quad[...] = total + dot(new, new)
        lu[0, after, now] = new
        return carry

    lax.fori_loop(0, NB, step, 0)
    for i in range(4):
        part = slice(i * 256, (i + 1) * 256)
        lu[1, part, N - B : N] = dot(tcol[part, :], w_ref[...]).astype(BF16)

    for d in others:
        s5_copy(d).wait_recv()
    raw = jnp.concatenate(
        [jnp.concatenate([pick[i, c] for i in range(8)], axis=0) for c in range(NB)], axis=1
    )
    for c in range(4):
        cols = slice(c * 256, (c + 1) * 256)
        deep = (c + 1) * 256
        low_w[:, cols] = dot(raw[:, :deep], lu[1, :deep, cols], NN).astype(BF16)
    for d in others:
        p_copy(d).wait_recv()
    for i in range(8):
        part = slice(i * B, (i + 1) * B)
        mine = jnp.concatenate([rows[c, part, :] for c in range(NB)], axis=1)
        for c in range(4):
            cols = slice(c * 256, (c + 1) * 256)
            deep = (c + 1) * 256
            fac[part, cols] = dot(mine[:, :deep], lu[1, :deep, cols], NN).astype(BF16)
        own_out[part, :] = fac[part, pl.ds(pl.multiple_of(z * B, B), B)]
        update = dot(fac[part, :], low_w[...])
        left = slab[part, :].astype(F32) - update
        for c in range(2):
            cols = slice(c * B, (c + 1) * B)
            slab_out[part, cols] = (left[:, cols] * pattern[i, c].astype(F32)).astype(BF16)

    for d in others:
        for g in range(4):
            y_copy(g, d).wait_send()
            q_copy(g, d).wait_send()
        c_copy(d).wait_send()
        p_copy(d).wait_send()
        s1_copy(d).wait_send()
        s2_copy(d).wait_send()
        s5_copy(d).wait_send()

        @pl.when(z == q)
        def _():
            s4_copy(d).wait_send()

    @pl.when(z != q)
    def _():
        s3_copy(z).wait_send()


def shards(pivot, panel, slab, pattern, col_source):
    vmem = pl.BlockSpec(memory_space=pltpu.VMEM)
    smem = pl.BlockSpec(memory_space=pltpu.SMEM)
    dma = pltpu.SemaphoreType.DMA
    return pl.pallas_call(
        kernel,
        out_shape=[
            jax.ShapeDtypeStruct((N, B), BF16),
            jax.ShapeDtypeStruct((N, 2 * B), BF16),
        ],
        in_specs=[vmem, vmem, vmem, smem, smem],
        out_specs=[vmem, vmem],
        scratch_shapes=[
            pltpu.VMEM((8, 32, 2, 16, B), BF16),
            pltpu.VMEM((8, 8, B), I32),
            pltpu.VMEM((8, 2 * B, B), BF16),
            pltpu.VMEM((8, 2 * B, B), BF16),
            pltpu.VMEM((8, 2 * B, B), BF16),
            pltpu.VMEM((9, 32, B), BF16),
            pltpu.VMEM((8, 8, 32, B), BF16),
            pltpu.VMEM((8, N, B), BF16),
            pltpu.VMEM((2, N, N), BF16),
            pltpu.VMEM((N, B), BF16),
            pltpu.VMEM((B, B), F32),
            pltpu.VMEM((B, B), BF16),
            pltpu.VMEM((2 * B, N), BF16),
            pltpu.VMEM((N, N), BF16),
            dma((4, 8)), dma((4, 8)), dma((4, 8)), dma((4, 8)),
            dma((8,)), dma((8,)), dma((8,)), dma((8,)),
            dma((8,)), dma((8,)), dma((8,)), dma((8,)),
            dma, dma((8,)),
            dma((8,)), dma((8,)), dma((8,)), dma((8,)),
        ],
        compiler_params=pltpu.CompilerParams(
            collective_id=0, has_side_effects=True, vmem_limit_bytes=56 * 2**20
        ),
        cost_estimate=pl.CostEstimate(
            flops=5 * 10**9, bytes_accessed=2 * 2**20, transcendentals=0
        ),
    )(pivot, panel, slab, pattern, col_source)


def solution(mesh):
    return jax.shard_map(
        shards,
        mesh=mesh,
        in_specs=(P("row", None), P("row", "col"), P("row", "col"), P("row", "col"), P("col")),
        out_specs=(P("row", "col"), P("row", "col")),
        check_vma=False,
    )
```

```python
import jax
import jax.numpy as jnp
from jax import lax
from jax.experimental import pallas as pl
from jax.experimental.pallas import tpu as pltpu
from jax.sharding import PartitionSpec as P

F32, BF16, I32 = jnp.float32, jnp.bfloat16, jnp.int32
B = 128
NB = 8
N = 1024
MESH = pl.DeviceIdType.MESH
NT = (((1,), (1,)), ((), ()))
NN = (((1,), (0,)), ((), ()))


def dot(a, b, dims=NT):
    return lax.dot_general(a, b, dims, preferred_element_type=F32)


def lane_spread(x, lane):
    return jnp.broadcast_to(x[:, lane : lane + 1], (8, B))


def row_spread(x, row):
    return jnp.broadcast_to(x[row : row + 1, :], (8, B))


def factor(rows, w_ref, aside):
    lane = lax.broadcasted_iota(I32, (8, B), 1)
    sub = lax.broadcasted_iota(I32, (8, B), 0)
    rows = list(rows)
    before = None
    cols = [lane_spread(rows[0], j) for j in range(8)]
    for p in range(16):
        more = p < 15
        if more:
            left = [lane_spread(rows[p + 1], 8 * p + j) for j in range(8)]
            ahead = [lane_spread(rows[p + 1], 8 * p + 8 + j) for j in range(8)]
        inside = (lane >= 8 * p) & (lane < 8 * p + 8)
        unit = jnp.where(lane == 8 * p + sub, 1.0, 0.0).astype(F32)
        low = jnp.where(inside, unit, rows[p])
        full = low
        inverse = jnp.zeros((8, B), F32)
        for k in range(8):
            inv = 1.0 / row_spread(cols[k], k)
            mult = cols[k] * inv
            both = jnp.where(sub == k, 0.0, mult)
            below = jnp.where(sub > k, mult, 0.0)
            across = [None] * 8
            for j in range(k + 1, 8):
                across[j] = row_spread(cols[j], k)
                cols[j] = cols[j] - both * across[j]
            if more:
                mult = left[k] * inv
                for j in range(8):
                    ahead[j] = ahead[j] - mult * row_spread(left[k], j)
                for j in range(k + 1, 8):
                    left[j] = left[j] - mult * across[j]
            full = full - both * row_spread(full, k)
            low = low - below * row_spread(low, k)
            inverse = jnp.where(sub == k, inv, inverse)
        w = jnp.where(lane < 8 * p + 8, low * jnp.sqrt(inverse), 0.0)
        if p % 2 == 0:
            before = w
        else:
            w_ref[8 * p - 8 : 8 * p + 8, :] = jnp.concatenate([before, w], 0).astype(BF16)
        full = full * inverse
        spread = [row_spread(full, k) for k in range(8)]
        for q in range(p + 1, 16):
            v = rows[q]
            t = [lane_spread(v, 8 * p + k) * spread[k] for k in range(8)]
            total = ((t[0] + t[1]) + (t[2] + t[3])) + ((t[4] + t[5]) + (t[6] + t[7]))
            rows[q] = jnp.where(inside, 0.0, v) - total
        if more:
            cols = ahead
        aside(p)


def kernel(
    pivot, panel, slab, pattern, col_source, own_out, slab_out,
    piv, cs, marked, part1, part2, part3, pick, rows, lu, tcol, quad, w_ref, low_w, fac,
    y_send, y_recv, q_send, q_recv, x_send, x_recv, k_send, k_recv, c_send, c_recv, p_send, p_recv,
    s1_send, s1_recv, s2_send, s2_recv, s3_send, s3_recv, s4_send, s4_recv, s5_send, s5_recv,
):
    r = lax.axis_index("row")
    z = lax.axis_index("col")
    x, y, core = r // 16, (r // 2) % 8, r % 2
    q = x * 2 + core

    def at_y(d):
        return ((x * 8 + (y + d) % 8) * 2 + core, z)

    def at_q(d):
        o = (q + d) % 8
        return (((o // 2) * 8 + y) * 2 + o % 2, z)

    def at_x(d):
        return ((((x + d) % 4) * 8 + y) * 2 + core, z)

    def at_z(d):
        return (r, (z + d) % 8)

    def remote(src, dst, send, recv, device):
        return pltpu.make_async_remote_copy(
            src_ref=src, dst_ref=dst, send_sem=send, recv_sem=recv,
            device_id=device, device_id_type=MESH,
        )

    def y_copy(g, d):
        ref = piv.at[0:1, x * 8 + y, core] if g == 0 else piv.at[1:8, x * 8 + y, core]
        return remote(ref, ref, y_send.at[g, d], y_recv.at[g, d], at_y(d))

    def q_copy(g, d):
        ref = piv.at[g : g + 1, pl.ds(x * 8, 8), core]
        return remote(ref, ref, q_send.at[g, d], q_recv.at[g, d], at_q(d))

    def x_copy(g, d):
        ref = piv.at[2 * g : 4 * g, pl.ds(x * 8, 8), core]
        return remote(ref, ref, x_send.at[g, d], x_recv.at[g, d], at_x(d))

    def k_copy(g):
        ref = piv.at[2 * g : 4 * g, :, core]
        return remote(ref, ref, k_send.at[g], k_recv.at[g], (r + 1 - 2 * core, z))

    def c_copy(d):
        ref = cs.at[z]
        return remote(ref, ref, c_send.at[d], c_recv.at[d], at_z(d))

    def p_copy(hop, way):
        if way == 0:
            block, device = (z + 8 - hop) % 8, (r, (z + 1) % 8)
        else:
            block, device = (z + hop) % 8, (r, (z + 7) % 8)
        if hop == 0:
            src, dst = panel, rows.at[z]
        elif hop < 3:
            src = dst = rows.at[block]
        else:
            src = dst = rows.at[block, way * (N // 2) : (way + 1) * (N // 2)]
        return remote(src, dst, p_send.at[hop, way], p_recv.at[hop, way], device)

    def p_hop(hop):
        for way in range(2):
            if hop:
                p_copy(hop - 1, way).wait_recv()
        for way in range(2):
            p_copy(hop, way).start()

    def s1_copy(d):
        return remote(
            marked.at[(q + d) % 8], part1.at[d], s1_send.at[d], s1_recv.at[d], at_q(d)
        )

    def s2_copy(d):
        return remote(
            part2.at[0, pl.ds(((y + d) % 8) * 32, 32)], part2.at[d, 0:32],
            s2_send.at[d], s2_recv.at[d], at_y(d),
        )

    def s3_copy(source):
        return remote(
            part3.at[0], part3.at[1 + source], s3_send, s3_recv.at[source], (r, q)
        )

    def s4_copy(d):
        ref = pick.at[y]
        return remote(ref, ref, s4_send.at[d], s4_recv.at[d], at_q(d))

    def s5_copy(d):
        ref = pick.at[y]
        return remote(ref, ref, s5_send.at[d], s5_recv.at[d], at_y(d))

    others = range(1, 8)

    barrier = pltpu.get_barrier_semaphore()
    for d in others:
        for device in (at_y(d), at_q(d), at_z(d)):
            pl.semaphore_signal(barrier, inc=1, device_id=device, device_id_type=MESH)

    for c in range(NB):
        piv[c, x * 8 + y, core] = pivot[:, c * B : (c + 1) * B].astype(BF16)
    sub = lax.broadcasted_iota(I32, (8, B), 0)
    cs[z] = jnp.where(sub == 0, col_source[0], col_source[1])

    pl.semaphore_wait(barrier, 21)
    for d in others:
        y_copy(0, d).start()
    for d in others:
        c_copy(d).start()
    for d in others:
        y_copy(1, d).start()
    p_hop(0)
    rows[z] = panel[...]
    lu[...] = jnp.zeros_like(lu)
    quad[...] = jnp.zeros_like(quad)
    tcol[...] = jnp.zeros_like(tcol)
    w_ref[...] = jnp.zeros_like(w_ref)
    for d in others:
        y_copy(0, d).wait_recv()
    for d in others:
        q_copy(0, d).start()

    for d in others:
        c_copy(d).wait_recv()

    def mark(pair, carry):
        for t in range(2):
            wanted = cs[pair, t : t + 1, :]
            total = jnp.zeros((B, B), F32)
            for s in range(8):
                here = panel[s * B : (s + 1) * B, :].astype(F32)
                total = jnp.where(wanted == r * 8 + s, here, total)
            marked[pair, t * B : (t + 1) * B, :] = total.astype(BF16)
        return carry

    lax.fori_loop(0, 8, mark, 0)
    for d in others:
        y_copy(1, d).wait_recv()
    for d in others:
        q_copy(1, d).start()
    for d in others:
        s1_copy(d).start()
    for g in (1, 2):
        for d in range(1, 4):
            x_copy(g, d).start()

    def block_rows(column, block):
        return piv[column, pl.ds(block * 4, 4)].reshape(B, B)

    def arrive(j):
        for g in range(2):
            @pl.when(j == g)
            def _():
                for d in others:
                    q_copy(g, d).wait_recv()

        @pl.when(j == 1)
        def _():
            p_hop(1)
            for d in range(1, 4):
                x_copy(1, d).wait_recv()
            k_copy(1).start()

        @pl.when(j == 2)
        def _():
            k_copy(1).wait_recv()

        @pl.when(j == 3)
        def _():
            p_hop(2)
            for d in range(1, 4):
                x_copy(2, d).wait_recv()
            k_copy(2).start()

        @pl.when(j == 4)
        def _():
            k_copy(2).wait_recv()

        @pl.when(j == 5)
        def _():
            p_hop(3)

        @pl.when(j == 1)
        def _():
            total = marked[q].astype(F32)
            for d in others:
                s1_copy(d).wait_recv()
            for d in others:
                total += part1[d].astype(F32)
            part2[0] = total.astype(BF16)
            for d in others:
                s2_copy(d).start()

        @pl.when(j == 2)
        def _():
            for d in others:
                s2_copy(d).wait_recv()
            total = part2[0, pl.ds(y * 32, 32), :].astype(F32)
            for d in others:
                total += part2[d, 0:32, :].astype(F32)
            part3[0] = total.astype(BF16)

            @pl.when(z != q)
            def _():
                s3_copy(z).start()

        @pl.when((j == 3) & (z == q))
        def _():
            for s in range(8):
                @pl.when(z != s)
                def _():
                    s3_copy(s).wait_recv()
                    pick[y, s] = part3[1 + s]
            pick[y, z] = part3[0]
            for d in others:
                s4_copy(d).start()

        @pl.when(j == 4)
        def _():
            for d in others:
                @pl.when((q + 8 - d) % 8 == z)
                def _():
                    s4_copy(d).wait_recv()
            for d in others:
                s5_copy(d).start()

    def step(j, carry):
        arrive(j)
        jm = jnp.maximum(j - 1, 0)
        jn = jnp.minimum(j + 1, NB - 1)
        now = pl.ds(pl.multiple_of(j * B, B), B)
        last = pl.ds(pl.multiple_of(jm * B, B), B)
        after = pl.ds(pl.multiple_of(jn * B, B), B)
        w_old = w_ref[...]
        row_j = lu[0, now, :]
        diagonal = block_rows(j, j).astype(F32) - quad[...]
        lu[0, after, last] = dot(tcol[after, :], w_old).astype(BF16)
        eye = jnp.where(
            lax.broadcasted_iota(I32, (B, B), 0) == lax.broadcasted_iota(I32, (B, B), 1), 1.0, 0.0
        ).astype(F32)

        def aside(p):
            block, half = p // 2, p % 2
            part = slice(p * 64, (p + 1) * 64)
            was_below = jnp.where(block > jm, 0, 1)
            done = dot(tcol[part, :], w_old).astype(BF16)
            lu[was_below, part, last] = done
            upper = jnp.where(block > j, 0, 1)
            t = -dot(lu[upper, part, :], row_j)
            source = piv[j, block * 4 + half * 2 : block * 4 + half * 2 + 2].reshape(64, B)
            on = jnp.where(block == j, 1.0, 0.0).astype(F32)
            t = t + jnp.where(block > j, source.astype(F32), 0.0) + eye[half * 64 : half * 64 + 64, :] * on
            tcol[part, :] = t.astype(BF16)
            if p == 3:
                row_next = lu[0, after, :]
                quad[...] = dot(row_next, row_next)

        factor([diagonal[8 * i : 8 * i + 8, :] for i in range(16)], w_ref, aside)
        new = dot(tcol[after, :], w_ref[...]).astype(BF16)
        quad[...] += dot(new, new)
        lu[0, after, now] = new
        return carry

    lax.fori_loop(0, NB, step, 0)
    for i in range(4):
        part = slice(i * 256, (i + 1) * 256)
        lu[1, part, N - B : N] = dot(tcol[part, :], w_ref[...]).astype(BF16)

    for d in others:
        s5_copy(d).wait_recv()
    raw = jnp.concatenate(
        [jnp.concatenate([pick[i, c] for i in range(8)], axis=0) for c in range(NB)], axis=1
    )
    for c in range(4):
        cols = slice(c * 256, (c + 1) * 256)
        deep = (c + 1) * 256
        low_w[:, cols] = dot(raw[:, :deep], lu[1, :deep, cols], NN).astype(BF16)
    for way in range(2):
        p_copy(3, way).wait_recv()
    for i in range(8):
        part = slice(i * B, (i + 1) * B)
        mine = jnp.concatenate([rows[c, part, :] for c in range(NB)], axis=1)
        for c in range(4):
            cols = slice(c * 256, (c + 1) * 256)
            deep = (c + 1) * 256
            fac[part, cols] = dot(mine[:, :deep], lu[1, :deep, cols], NN).astype(BF16)
        own_out[part, :] = fac[part, pl.ds(pl.multiple_of(z * B, B), B)]
        update = dot(fac[part, :], low_w[...])
        left = slab[part, :].astype(F32) - update
        for c in range(2):
            cols = slice(c * B, (c + 1) * B)
            slab_out[part, cols] = (left[:, cols] * pattern[i, c].astype(F32)).astype(BF16)

    for g in range(1, 3):
        for d in range(1, 4):
            x_copy(g, d).wait_send()
        k_copy(g).wait_send()
    for hop in range(4):
        for way in range(2):
            p_copy(hop, way).wait_send()
    for d in others:
        for g in range(2):
            y_copy(g, d).wait_send()
            q_copy(g, d).wait_send()
        c_copy(d).wait_send()
        s1_copy(d).wait_send()
        s2_copy(d).wait_send()
        s5_copy(d).wait_send()

        @pl.when(z == q)
        def _():
            s4_copy(d).wait_send()

    @pl.when(z != q)
    def _():
        s3_copy(z).wait_send()


def shards(pivot, panel, slab, pattern, col_source):
    vmem = pl.BlockSpec(memory_space=pltpu.VMEM)
    smem = pl.BlockSpec(memory_space=pltpu.SMEM)
    dma = pltpu.SemaphoreType.DMA
    return pl.pallas_call(
        kernel,
        out_shape=[
            jax.ShapeDtypeStruct((N, B), BF16),
            jax.ShapeDtypeStruct((N, 2 * B), BF16),
        ],
        in_specs=[vmem, vmem, vmem, smem, smem],
        out_specs=[vmem, vmem],
        scratch_shapes=[
            pltpu.VMEM((8, 32, 2, 16, B), BF16),
            pltpu.VMEM((8, 8, B), I32),
            pltpu.VMEM((8, 2 * B, B), BF16),
            pltpu.VMEM((8, 2 * B, B), BF16),
            pltpu.VMEM((8, 2 * B, B), BF16),
            pltpu.VMEM((9, 32, B), BF16),
            pltpu.VMEM((8, 8, 32, B), BF16),
            pltpu.VMEM((8, N, B), BF16),
            pltpu.VMEM((2, N, N), BF16),
            pltpu.VMEM((N, B), BF16),
            pltpu.VMEM((B, B), F32),
            pltpu.VMEM((B, B), BF16),
            pltpu.VMEM((2 * B, N), BF16),
            pltpu.VMEM((N, N), BF16),
            dma((2, 8)), dma((2, 8)), dma((2, 8)), dma((2, 8)),
            dma((3, 4)), dma((3, 4)), dma((3,)), dma((3,)),
            dma((8,)), dma((8,)), dma((4, 2)), dma((4, 2)),
            dma((8,)), dma((8,)), dma((8,)), dma((8,)),
            dma, dma((8,)),
            dma((8,)), dma((8,)), dma((8,)), dma((8,)),
        ],
        compiler_params=pltpu.CompilerParams(
            collective_id=0, has_side_effects=True, vmem_limit_bytes=56 * 2**20
        ),
        cost_estimate=pl.CostEstimate(
            flops=5 * 10**9, bytes_accessed=2 * 2**20, transcendentals=0
        ),
    )(pivot, panel, slab, pattern, col_source)


def solution(mesh):
    return jax.shard_map(
        shards,
        mesh=mesh,
        in_specs=(P("row", None), P("row", "col"), P("row", "col"), P("row", "col"), P("col")),
        out_specs=(P("row", "col"), P("row", "col")),
        check_vma=False,
    )
```

```python
import jax
import jax.numpy as jnp
from jax import lax
from jax.experimental import pallas as pl
from jax.experimental.pallas import tpu as pltpu
from jax.sharding import PartitionSpec as P

F32, BF16, I32 = jnp.float32, jnp.bfloat16, jnp.int32
B = 128
NB = 8
N = 1024
MESH = pl.DeviceIdType.MESH
GROUPS = (slice(0, 1), slice(1, 2), slice(2, 4), slice(4, 8))
NT = (((1,), (1,)), ((), ()))
NN = (((1,), (0,)), ((), ()))


def dot(a, b, dims=NT):
    return lax.dot_general(a, b, dims, preferred_element_type=F32)


def lane_spread(x, lane):
    return jnp.broadcast_to(x[:, lane : lane + 1], (8, B))


def row_spread(x, row):
    return jnp.broadcast_to(x[row : row + 1, :], (8, B))


def factor(rows, w_ref, aside):
    lane = lax.broadcasted_iota(I32, (8, B), 1)
    sub = lax.broadcasted_iota(I32, (8, B), 0)
    rows = list(rows)
    before = None
    cols = [lane_spread(rows[0], j) for j in range(8)]
    for p in range(16):
        more = p < 15
        if more:
            left = [lane_spread(rows[p + 1], 8 * p + j) for j in range(8)]
            ahead = [lane_spread(rows[p + 1], 8 * p + 8 + j) for j in range(8)]
        inside = (lane >= 8 * p) & (lane < 8 * p + 8)
        unit = jnp.where(lane == 8 * p + sub, 1.0, 0.0).astype(F32)
        low = jnp.where(inside, unit, rows[p])
        full = low
        inverse = jnp.zeros((8, B), F32)
        for k in range(8):
            inv = 1.0 / row_spread(cols[k], k)
            mult = cols[k] * inv
            both = jnp.where(sub == k, 0.0, mult)
            below = jnp.where(sub > k, mult, 0.0)
            across = [None] * 8
            for j in range(k + 1, 8):
                across[j] = row_spread(cols[j], k)
                cols[j] = cols[j] - both * across[j]
            if more:
                mult = left[k] * inv
                for j in range(8):
                    ahead[j] = ahead[j] - mult * row_spread(left[k], j)
                for j in range(k + 1, 8):
                    left[j] = left[j] - mult * across[j]
            full = full - both * row_spread(full, k)
            low = low - below * row_spread(low, k)
            inverse = jnp.where(sub == k, inv, inverse)
        w = jnp.where(lane < 8 * p + 8, low * jnp.sqrt(inverse), 0.0)
        if p % 2 == 0:
            before = w
        else:
            w_ref[8 * p - 8 : 8 * p + 8, :] = jnp.concatenate([before, w], 0).astype(BF16)
        full = full * inverse
        spread = [row_spread(full, k) for k in range(8)]
        for q in range(p + 1, 16):
            v = rows[q]
            t = [lane_spread(v, 8 * p + k) * spread[k] for k in range(8)]
            total = ((t[0] + t[1]) + (t[2] + t[3])) + ((t[4] + t[5]) + (t[6] + t[7]))
            rows[q] = jnp.where(inside, 0.0, v) - total
        if more:
            cols = ahead
        aside(p)


def kernel(
    pivot, panel, slab, pattern, col_source, own_out, slab_out,
    piv, cs, marked, part1, part2, part3, held, pick, rows, lu, tcol, quad, w_ref, low_w, fac,
    y_send, y_recv, x_send, x_recv, k_send, k_recv, c_send, c_recv, p_send, p_recv,
    s1_send, s1_recv, s2_send, s2_recv, s3_send, s3_recv, s4_send, s4_recv, s5_send, s5_recv, s6_send, s6_recv,
):
    r = lax.axis_index("row")
    z = lax.axis_index("col")
    x, y, core = r // 16, (r // 2) % 8, r % 2
    q = x * 2 + core

    def at_y(d):
        return ((x * 8 + (y + d) % 8) * 2 + core, z)

    def at_q(d):
        o = (q + d) % 8
        return (((o // 2) * 8 + y) * 2 + o % 2, z)

    def at_x(d):
        return ((((x + d) % 4) * 8 + y) * 2 + core, z)

    def at_z(d):
        return (r, (z + d) % 8)

    def remote(src, dst, send, recv, device):
        return pltpu.make_async_remote_copy(
            src_ref=src, dst_ref=dst, send_sem=send, recv_sem=recv,
            device_id=device, device_id_type=MESH,
        )

    def y_copy(g, d):
        ref = piv.at[GROUPS[g], :, y, core] if g == 2 else piv.at[GROUPS[g], x, y, core]
        return remote(ref, ref, y_send.at[g, d], y_recv.at[g, d], at_y(d))

    def x_copy(g, d):
        ref = piv.at[GROUPS[g], x, y, core] if g == 2 else piv.at[GROUPS[g], x, :, core]
        return remote(ref, ref, x_send.at[g, d], x_recv.at[g, d], at_x(d))

    def k_copy(g):
        ref = piv.at[GROUPS[g], :, :, core]
        return remote(ref, ref, k_send.at[g], k_recv.at[g], (r + 1 - 2 * core, z))

    def c_copy(d):
        ref = cs.at[z]
        return remote(ref, ref, c_send.at[d], c_recv.at[d], at_z(d))

    def p_copy(hop, way):
        if way == 0:
            block, device = (z + 8 - hop) % 8, (r, (z + 1) % 8)
        else:
            block, device = (z + hop) % 8, (r, (z + 7) % 8)
        if hop == 0:
            src, dst = panel, rows.at[z]
        elif hop < 3:
            src = dst = rows.at[block]
        else:
            src = dst = rows.at[block, way * (N // 2) : (way + 1) * (N // 2)]
        return remote(src, dst, p_send.at[hop, way], p_recv.at[hop, way], device)

    def p_hop(hop):
        for way in range(2):
            if hop:
                p_copy(hop - 1, way).wait_recv()
        for way in range(2):
            p_copy(hop, way).start()

    def s1_copy(d):
        return remote(
            marked.at[(q + d) % 8], part1.at[d], s1_send.at[d], s1_recv.at[d], at_q(d)
        )

    def s2_copy(d):
        return remote(
            part2.at[0, pl.ds(((y + d) % 8) * 32, 32)], part2.at[d, 0:32],
            s2_send.at[d], s2_recv.at[d], at_y(d),
        )

    def s3_copy(source):
        return remote(
            part3.at[0], part3.at[1 + source], s3_send, s3_recv.at[source], (r, q)
        )

    def s4_copy(d):
        half = (q + d) % 2
        return remote(
            held.at[pl.ds(half * 4, 4)], pick.at[y, pl.ds(half * 4, 4)],
            s4_send.at[d], s4_recv.at[d], at_q(d),
        )

    def s5_copy(d):
        ref = pick.at[y, pl.ds(core * 4, 4)]
        return remote(ref, ref, s5_send.at[d], s5_recv.at[d], at_y(d))

    def s6_copy():
        ref = pick.at[:, pl.ds(core * 4, 4)]
        return remote(ref, ref, s6_send, s6_recv, (r + 1 - 2 * core, z))

    others = range(1, 8)

    barrier = pltpu.get_barrier_semaphore()
    for d in others:
        for device in (at_y(d), at_q(d), at_z(d)):
            pl.semaphore_signal(barrier, inc=1, device_id=device, device_id_type=MESH)

    for c in range(NB):
        piv[c, x, y, core] = pivot[:, c * B : (c + 1) * B].astype(BF16)
    sub = lax.broadcasted_iota(I32, (8, B), 0)
    cs[z] = jnp.where(sub == 0, col_source[0], col_source[1])

    pl.semaphore_wait(barrier, 21)
    for d in others:
        y_copy(0, d).start()
    for d in others:
        c_copy(d).start()
    for d in range(1, 4):
        x_copy(2, d).start()
    for g in (1, 3):
        for d in others:
            y_copy(g, d).start()
    rows[z] = panel[...]
    lu[...] = jnp.zeros_like(lu)
    quad[...] = jnp.zeros_like(quad)
    tcol[...] = jnp.zeros_like(tcol)
    w_ref[...] = jnp.zeros_like(w_ref)
    for g in (0, 1):
        for d in others:
            y_copy(g, d).wait_recv()
        for d in range(1, 4):
            x_copy(g, d).start()

    for d in others:
        c_copy(d).wait_recv()

    def mark(pair, carry):
        for t in range(2):
            wanted = cs[pair, t : t + 1, :]
            total = jnp.zeros((B, B), F32)
            for s in range(8):
                here = panel[s * B : (s + 1) * B, :].astype(F32)
                total = jnp.where(wanted == r * 8 + s, here, total)
            marked[pair, t * B : (t + 1) * B, :] = total.astype(BF16)
        return carry

    lax.fori_loop(0, 8, mark, 0)
    for d in others:
        s1_copy(d).start()
    for d in range(1, 4):
        x_copy(2, d).wait_recv()
    for d in others:
        y_copy(2, d).start()
    p_hop(0)
    for g in (0, 1):
        for d in range(1, 4):
            x_copy(g, d).wait_recv()
        k_copy(g).start()

    def block_rows(column, block):
        return piv[column, block // 2, pl.ds((block % 2) * 4, 4)].reshape(B, B)

    def s1_on():
        total = marked[q].astype(F32)
        for d in others:
            s1_copy(d).wait_recv()
        for d in others:
            total += part1[d].astype(F32)
        part2[0] = total.astype(BF16)
        for d in others:
            s2_copy(d).start()

    def s2_on():
        for d in others:
            s2_copy(d).wait_recv()
        total = part2[0, pl.ds(y * 32, 32), :].astype(F32)
        for d in others:
            total += part2[d, 0:32, :].astype(F32)
        part3[0] = total.astype(BF16)

        @pl.when(z != q)
        def _():
            s3_copy(z).start()

    def s3_on():
        @pl.when(z == q)
        def _():
            for s in range(8):
                @pl.when(z != s)
                def _():
                    s3_copy(s).wait_recv()
                    held[s] = part3[1 + s]
            held[z] = part3[0]
            pick[y, pl.ds(core * 4, 4)] = held[pl.ds(core * 4, 4)]
            for d in others:
                s4_copy(d).start()

    def s4_on():
        for d in others:
            @pl.when((q + 8 - d) % 8 == z)
            def _():
                s4_copy(d).wait_recv()
        for d in others:
            s5_copy(d).start()

    def s5_on():
        for d in others:
            s5_copy(d).wait_recv()
        s6_copy().start()

    def y2_on():
        for d in others:
            y_copy(2, d).wait_recv()
        k_copy(2).start()

    def y3_on():
        for d in others:
            y_copy(3, d).wait_recv()
        for d in range(1, 4):
            x_copy(3, d).start()

    def x3_on():
        for d in range(1, 4):
            x_copy(3, d).wait_recv()
        k_copy(3).start()

    plan = {
        0: [lambda: k_copy(0).wait_recv()],
        1: [y3_on],
        2: [lambda: k_copy(1).wait_recv(), y2_on],
        3: [s1_on],
        4: [lambda: k_copy(2).wait_recv(), lambda: p_hop(1)],
        5: [x3_on],
        6: [s2_on],
        8: [lambda: k_copy(3).wait_recv(), lambda: p_hop(2), s3_on],
        11: [s4_on],
        12: [lambda: p_hop(3)],
        15: [s5_on],
    }

    def arrive(j, half):
        for at, parts in plan.items():
            if at % 2 == half:
                @pl.when(j == at // 2)
                def _():
                    for part in parts:
                        part()

    def step(j, carry):
        arrive(j, 0)
        jm = jnp.maximum(j - 1, 0)
        jn = jnp.minimum(j + 1, NB - 1)
        now = pl.ds(pl.multiple_of(j * B, B), B)
        last = pl.ds(pl.multiple_of(jm * B, B), B)
        after = pl.ds(pl.multiple_of(jn * B, B), B)
        w_old = w_ref[...]
        row_j = lu[0, now, :]
        diagonal = block_rows(j, j).astype(F32) - quad[...]
        lu[0, after, last] = dot(tcol[after, :], w_old).astype(BF16)
        eye = jnp.where(
            lax.broadcasted_iota(I32, (B, B), 0) == lax.broadcasted_iota(I32, (B, B), 1), 1.0, 0.0
        ).astype(F32)

        def aside(p):
            block, half = p // 2, p % 2
            part = slice(p * 64, (p + 1) * 64)
            was_below = jnp.where(block > jm, 0, 1)
            done = dot(tcol[part, :], w_old).astype(BF16)
            lu[was_below, part, last] = done
            upper = jnp.where(block > j, 0, 1)
            t = -dot(lu[upper, part, :], row_j)
            low = (block % 2) * 4 + half * 2
            source = piv[j, block // 2, low : low + 2].reshape(64, B)
            on = jnp.where(block == j, 1.0, 0.0).astype(F32)
            t = t + jnp.where(block > j, source.astype(F32), 0.0) + eye[half * 64 : half * 64 + 64, :] * on
            tcol[part, :] = t.astype(BF16)
            if p == 7:
                arrive(j, 1)
            if p == 3:
                row_next = lu[0, after, :]
                quad[...] = dot(row_next, row_next)

        factor([diagonal[8 * i : 8 * i + 8, :] for i in range(16)], w_ref, aside)
        new = dot(tcol[after, :], w_ref[...]).astype(BF16)
        quad[...] += dot(new, new)
        lu[0, after, now] = new
        return carry

    lax.fori_loop(0, NB, step, 0)
    for i in range(4):
        part = slice(i * 256, (i + 1) * 256)
        lu[1, part, N - B : N] = dot(tcol[part, :], w_ref[...]).astype(BF16)

    for way in range(2):
        p_copy(3, way).wait_recv()
    for i in range(8):
        part = slice(i * B, (i + 1) * B)
        mine = jnp.concatenate([rows[c, part, :] for c in range(NB)], axis=1)
        for c in range(4):
            cols = slice(c * 256, (c + 1) * 256)
            deep = (c + 1) * 256
            fac[part, cols] = dot(mine[:, :deep], lu[1, :deep, cols], NN).astype(BF16)
        own_out[part, :] = fac[part, pl.ds(pl.multiple_of(z * B, B), B)]

    s6_copy().wait_recv()
    raw = jnp.concatenate(
        [jnp.concatenate([pick[i, c] for i in range(8)], axis=0) for c in range(NB)], axis=1
    )
    for c in range(4):
        cols = slice(c * 256, (c + 1) * 256)
        deep = (c + 1) * 256
        low_w[:, cols] = dot(raw[:, :deep], lu[1, :deep, cols], NN).astype(BF16)
    for i in range(8):
        part = slice(i * B, (i + 1) * B)
        update = dot(fac[part, :], low_w[...])
        left = slab[part, :].astype(F32) - update
        for c in range(2):
            cols = slice(c * B, (c + 1) * B)
            slab_out[part, cols] = (left[:, cols] * pattern[i, c].astype(F32)).astype(BF16)

    for g in range(4):
        for d in others:
            y_copy(g, d).wait_send()
        for d in range(1, 4):
            x_copy(g, d).wait_send()
        k_copy(g).wait_send()
    for hop in range(4):
        for way in range(2):
            p_copy(hop, way).wait_send()
    for d in others:
        c_copy(d).wait_send()
        s1_copy(d).wait_send()
        s2_copy(d).wait_send()
        s5_copy(d).wait_send()

        @pl.when(z == q)
        def _():
            s4_copy(d).wait_send()

    s6_copy().wait_send()

    @pl.when(z != q)
    def _():
        s3_copy(z).wait_send()


def shards(pivot, panel, slab, pattern, col_source):
    vmem = pl.BlockSpec(memory_space=pltpu.VMEM)
    smem = pl.BlockSpec(memory_space=pltpu.SMEM)
    dma = pltpu.SemaphoreType.DMA
    return pl.pallas_call(
        kernel,
        out_shape=[
            jax.ShapeDtypeStruct((N, B), BF16),
            jax.ShapeDtypeStruct((N, 2 * B), BF16),
        ],
        in_specs=[vmem, vmem, vmem, smem, smem],
        out_specs=[vmem, vmem],
        scratch_shapes=[
            pltpu.VMEM((8, 4, 8, 2, 16, B), BF16),
            pltpu.VMEM((8, 8, B), I32),
            pltpu.VMEM((8, 2 * B, B), BF16),
            pltpu.VMEM((8, 2 * B, B), BF16),
            pltpu.VMEM((8, 2 * B, B), BF16),
            pltpu.VMEM((9, 32, B), BF16),
            pltpu.VMEM((8, 32, B), BF16),
            pltpu.VMEM((8, 8, 32, B), BF16),
            pltpu.VMEM((8, N, B), BF16),
            pltpu.VMEM((2, N, N), BF16),
            pltpu.VMEM((N, B), BF16),
            pltpu.VMEM((B, B), F32),
            pltpu.VMEM((B, B), BF16),
            pltpu.VMEM((2 * B, N), BF16),
            pltpu.VMEM((N, N), BF16),
            dma((4, 8)), dma((4, 8)), dma((4, 4)), dma((4, 4)), dma((4,)), dma((4,)),
            dma((8,)), dma((8,)), dma((4, 2)), dma((4, 2)),
            dma((8,)), dma((8,)), dma((8,)), dma((8,)),
            dma, dma((8,)),
            dma((8,)), dma((8,)), dma((8,)), dma((8,)), dma, dma,
        ],
        compiler_params=pltpu.CompilerParams(
            collective_id=0, has_side_effects=True, vmem_limit_bytes=56 * 2**20
        ),
        cost_estimate=pl.CostEstimate(
            flops=5 * 10**9, bytes_accessed=2 * 2**20, transcendentals=0
        ),
    )(pivot, panel, slab, pattern, col_source)


def solution(mesh):
    return jax.shard_map(
        shards,
        mesh=mesh,
        in_specs=(P("row", None), P("row", "col"), P("row", "col"), P("row", "col"), P("col")),
        out_specs=(P("row", "col"), P("row", "col")),
        check_vma=False,
    )
```

```python
import jax
import jax.numpy as jnp
from jax import lax
from jax.experimental import pallas as pl
from jax.experimental.pallas import tpu as pltpu
from jax.sharding import PartitionSpec as P

F32, BF16, I32 = jnp.float32, jnp.bfloat16, jnp.int32
B = 128
NB = 8
N = 1024
MESH = pl.DeviceIdType.MESH
GROUPS = (slice(0, 1), slice(1, 2), slice(2, 4), slice(4, 8))
ASIDES = (
    (0, ("finish", (0, 1, 2, 3))),
    (1, ("finish", (4, 5, 6, 7))),
    (4, ("begin", (0,))),
    (5, ("begin", (1,))),
    (6, ("begin", (2,))),
    (7, ("begin", (3,))),
    (9, ("begin", (4,))),
    (10, ("begin", (5,))),
    (11, ("begin", (6,))),
    (12, ("begin", (7,))),
)
NT = (((1,), (1,)), ((), ()))
NN = (((1,), (0,)), ((), ()))


def dot(a, b, dims=NT):
    return lax.dot_general(a, b, dims, preferred_element_type=F32)


def lane_spread(x, lane):
    return jnp.broadcast_to(x[:, lane : lane + 1], (8, B))


def row_spread(x, row):
    return jnp.broadcast_to(x[row : row + 1, :], (8, B))


def factor(rows, w_ref, aside):
    lane = lax.broadcasted_iota(I32, (8, B), 1)
    sub = lax.broadcasted_iota(I32, (8, B), 0)
    rows = list(rows)
    before = None
    cols = [lane_spread(rows[0], j) for j in range(8)]
    for p in range(16):
        more = p < 15
        if more:
            left = [lane_spread(rows[p + 1], 8 * p + j) for j in range(8)]
            ahead = [lane_spread(rows[p + 1], 8 * p + 8 + j) for j in range(8)]
        inside = (lane >= 8 * p) & (lane < 8 * p + 8)
        unit = jnp.where(lane == 8 * p + sub, 1.0, 0.0).astype(F32)
        low = jnp.where(inside, unit, rows[p])
        full = low
        inverse = jnp.zeros((8, B), F32)
        for k in range(8):
            inv = 1.0 / row_spread(cols[k], k)
            mult = cols[k] * inv
            both = jnp.where(sub == k, 0.0, mult)
            below = jnp.where(sub > k, mult, 0.0)
            across = [None] * 8
            for j in range(k + 1, 8):
                across[j] = row_spread(cols[j], k)
                cols[j] = cols[j] - both * across[j]
            if more:
                mult = left[k] * inv
                for j in range(8):
                    ahead[j] = ahead[j] - mult * row_spread(left[k], j)
                for j in range(k + 1, 8):
                    left[j] = left[j] - mult * across[j]
            full = full - both * row_spread(full, k)
            low = low - below * row_spread(low, k)
            inverse = jnp.where(sub == k, inv, inverse)
        w = jnp.where(lane < 8 * p + 8, low * jnp.sqrt(inverse), 0.0)
        if p % 2 == 0:
            before = w
        else:
            w_ref[8 * p - 8 : 8 * p + 8, :] = jnp.concatenate([before, w], 0).astype(BF16)
        full = full * inverse
        spread = [row_spread(full, k) for k in range(8)]
        for q in range(p + 1, min(p + 3, 16)):
            v = rows[q]
            t = [lane_spread(v, 8 * p + k) * spread[k] for k in range(8)]
            total = ((t[0] + t[1]) + (t[2] + t[3])) + ((t[4] + t[5]) + (t[6] + t[7]))
            rows[q] = jnp.where(inside, 0.0, v) - total
        if p < 13:
            far = jnp.concatenate(rows[p + 3 :], 0) if p < 12 else rows[15]
            zero = jnp.zeros((8, B), F32)
            padded = jnp.concatenate([zero] * p + [full] + [zero] * (15 - p), 0).astype(BF16)
            total = dot(far.astype(BF16), padded, NN)
            for i, q in enumerate(range(p + 3, 16)):
                rows[q] = jnp.where(inside, 0.0, rows[q]) - total[8 * i : 8 * i + 8]
        if more:
            cols = ahead
        aside(p)


def kernel(
    pivot, panel, slab, pattern, col_source, own_out, slab_out,
    piv, cs, marked, part0, chip, part1, part2, part3, held, pick, rows, lu, tcol, quad, w_ref, low_w, fac,
    y_send, y_recv, x_send, x_recv, k_send, k_recv, c_send, c_recv, p_send, p_recv,
    s1_send, s1_recv, s2_send, s2_recv, s3_send, s3_recv, s4_send, s4_recv, s5_send, s5_recv, s6_send, s6_recv, s0_send, s0_recv,
):
    r = lax.axis_index("row")
    z = lax.axis_index("col")
    x, y, core = r // 16, (r // 2) % 8, r % 2
    q = x * 2 + core

    def at_y(d):
        return ((x * 8 + (y + d) % 8) * 2 + core, z)

    def at_q(d):
        o = (q + d) % 8
        return (((o // 2) * 8 + y) * 2 + o % 2, z)

    def at_x(d):
        return ((((x + d) % 4) * 8 + y) * 2 + core, z)

    def at_z(d):
        return (r, (z + d) % 8)

    def remote(src, dst, send, recv, device):
        return pltpu.make_async_remote_copy(
            src_ref=src, dst_ref=dst, send_sem=send, recv_sem=recv,
            device_id=device, device_id_type=MESH,
        )

    def y_copy(g, d):
        ref = piv.at[GROUPS[g], :, y, core] if g == 2 else piv.at[GROUPS[g], x, y, core]
        return remote(ref, ref, y_send.at[g, d], y_recv.at[g, d], at_y(d))

    def x_copy(g, d):
        ref = piv.at[GROUPS[g], x, y, core] if g == 2 else piv.at[GROUPS[g], x, :, core]
        return remote(ref, ref, x_send.at[g, d], x_recv.at[g, d], at_x(d))

    def k_copy(g):
        ref = piv.at[GROUPS[g], :, :, core]
        return remote(ref, ref, k_send.at[g], k_recv.at[g], (r + 1 - 2 * core, z))

    def c_copy(d):
        ref = cs.at[z]
        return remote(ref, ref, c_send.at[d], c_recv.at[d], at_z(d))

    def p_copy(hop, way):
        if way == 0:
            block, device = (z + 8 - hop) % 8, (r, (z + 1) % 8)
        else:
            block, device = (z + hop) % 8, (r, (z + 7) % 8)
        if hop == 0:
            src, dst = panel, rows.at[z]
        elif hop < 3:
            src = dst = rows.at[block]
        else:
            src = dst = rows.at[block, way * (N // 2) : (way + 1) * (N // 2)]
        return remote(src, dst, p_send.at[hop, way], p_recv.at[hop, way], device)

    def p_hop(hop):
        for way in range(2):
            if hop:
                p_copy(hop - 1, way).wait_recv()
        for way in range(2):
            p_copy(hop, way).start()

    def s0_copy():
        return remote(
            marked.at[:, 1 - core], part0, s0_send, s0_recv, (r + 1 - 2 * core, z)
        )

    def s1_copy(d):
        return remote(
            chip.at[(x + d) % 4], part1.at[d], s1_send.at[d], s1_recv.at[d], at_x(d)
        )

    def s2_copy(d):
        return remote(
            part2.at[0, pl.ds(((y + d) % 8) * 32, 32)], part2.at[d, 0:32],
            s2_send.at[d], s2_recv.at[d], at_y(d),
        )

    def s3_copy(source):
        return remote(
            part3.at[0], part3.at[1 + source], s3_send, s3_recv.at[source], (r, q)
        )

    def s4_copy(d):
        half = (q + d) % 2
        return remote(
            held.at[pl.ds(half * 4, 4)], pick.at[y, pl.ds(half * 4, 4)],
            s4_send.at[d], s4_recv.at[d], at_q(d),
        )

    def s5_copy(d):
        ref = pick.at[y, pl.ds(core * 4, 4)]
        return remote(ref, ref, s5_send.at[d], s5_recv.at[d], at_y(d))

    def s6_copy():
        ref = pick.at[:, pl.ds(core * 4, 4)]
        return remote(ref, ref, s6_send, s6_recv, (r + 1 - 2 * core, z))

    others = range(1, 8)

    barrier = pltpu.get_barrier_semaphore()
    for d in others:
        for device in (at_y(d), at_q(d), at_z(d)):
            pl.semaphore_signal(barrier, inc=1, device_id=device, device_id_type=MESH)

    for c in range(NB):
        piv[c, x, y, core] = pivot[:, c * B : (c + 1) * B].astype(BF16)
    sub = lax.broadcasted_iota(I32, (8, B), 0)
    cs[z] = jnp.where(sub == 0, col_source[0], col_source[1])

    pl.semaphore_wait(barrier, 21)
    for d in others:
        y_copy(0, d).start()
    for d in others:
        c_copy(d).start()
    for d in range(1, 4):
        x_copy(2, d).start()
    for g in (1, 3):
        for d in others:
            y_copy(g, d).start()
    p_hop(0)
    rows[z] = panel[...]
    lu[...] = jnp.zeros_like(lu)
    quad[...] = jnp.zeros_like(quad)
    tcol[...] = jnp.zeros_like(tcol)
    w_ref[...] = jnp.zeros_like(w_ref)
    for d in others:
        y_copy(0, d).wait_recv()
    for d in range(1, 4):
        x_copy(0, d).start()

    for d in others:
        c_copy(d).wait_recv()

    def mark(pair, carry):
        for t in range(2):
            wanted = cs[pair, t : t + 1, :]
            total = jnp.zeros((B, B), F32)
            for s in range(8):
                here = panel[s * B : (s + 1) * B, :].astype(F32)
                total = jnp.where(wanted == r * 8 + s, here, total)
            marked[pair // 2, pair % 2, t * B : (t + 1) * B, :] = total.astype(BF16)
        return carry

    lax.fori_loop(0, 8, mark, 0)
    s0_copy().start()
    for d in others:
        y_copy(1, d).wait_recv()
    for d in range(1, 4):
        x_copy(1, d).start()
    for d in range(1, 4):
        x_copy(2, d).wait_recv()
    for d in others:
        y_copy(2, d).start()
    for d in range(1, 4):
        x_copy(0, d).wait_recv()
    k_copy(0).start()
    s0_copy().wait_recv()
    for i in range(4):
        chip[i] = marked[i, core] + part0[i]
    for d in range(1, 4):
        s1_copy(d).start()
    for d in range(1, 4):
        x_copy(1, d).wait_recv()
    k_copy(1).start()

    def block_rows(column, block):
        return piv[column, block // 2, pl.ds((block % 2) * 4, 4)].reshape(B, B)

    def s1_on():
        total = chip[x].astype(F32)
        for d in range(1, 4):
            s1_copy(d).wait_recv()
        for d in range(1, 4):
            total += part1[d].astype(F32)
        part2[0] = total.astype(BF16)
        for d in others:
            s2_copy(d).start()

    def s2_on():
        for d in others:
            s2_copy(d).wait_recv()
        total = part2[0, pl.ds(y * 32, 32), :].astype(F32)
        for d in others:
            total += part2[d, 0:32, :].astype(F32)
        part3[0] = total.astype(BF16)

        @pl.when(z != q)
        def _():
            s3_copy(z).start()

    def s3_on():
        @pl.when(z == q)
        def _():
            for s in range(8):
                @pl.when(z != s)
                def _():
                    s3_copy(s).wait_recv()
                    held[s] = part3[1 + s]
            held[z] = part3[0]
            pick[y, pl.ds(core * 4, 4)] = held[pl.ds(core * 4, 4)]
            for d in others:
                s4_copy(d).start()

    def s4_on():
        for d in others:
            @pl.when((q + 8 - d) % 8 == z)
            def _():
                s4_copy(d).wait_recv()
        for d in others:
            s5_copy(d).start()

    def s5_on():
        for d in others:
            s5_copy(d).wait_recv()
        s6_copy().start()

    def y2_on():
        for d in others:
            y_copy(2, d).wait_recv()
        k_copy(2).start()

    def y3_on():
        for d in others:
            y_copy(3, d).wait_recv()
        for d in range(1, 4):
            x_copy(3, d).start()

    def x3_on():
        for d in range(1, 4):
            x_copy(3, d).wait_recv()
        k_copy(3).start()

    plan = {
        0: [lambda: k_copy(0).wait_recv()],
        1: [lambda: p_hop(1)],
        2: [y3_on],
        4: [lambda: k_copy(1).wait_recv()],
        5: [y2_on],
        6: [s1_on],
        8: [lambda: k_copy(2).wait_recv()],
        12: [s2_on],
        13: [x3_on, lambda: p_hop(2)],
        16: [lambda: k_copy(3).wait_recv(), s3_on],
        22: [s4_on],
        24: [lambda: p_hop(3)],
    }

    def arrive(j, quarter):
        for at, parts in plan.items():
            if at % 4 == quarter:
                @pl.when(j == at // 4)
                def _():
                    for part in parts:
                        part()

    def step(j, carry):
        arrive(j, 0)
        jm = jnp.maximum(j - 1, 0)
        jn = jnp.minimum(j + 1, NB - 1)
        now = pl.ds(pl.multiple_of(j * B, B), B)
        last = pl.ds(pl.multiple_of(jm * B, B), B)
        after = pl.ds(pl.multiple_of(jn * B, B), B)
        w_old = w_ref[...]
        row_j = lu[0, now, :]
        diagonal = block_rows(j, j).astype(F32) - quad[...]
        lu[0, after, last] = dot(tcol[after, :], w_old).astype(BF16)
        eye = jnp.where(
            lax.broadcasted_iota(I32, (B, B), 0) == lax.broadcasted_iota(I32, (B, B), 1), 1.0, 0.0
        ).astype(F32)

        def finish(blocks):
            done = dot(tcol[blocks[0] * B : (blocks[-1] + 1) * B, :], w_old).astype(BF16)
            for i, block in enumerate(blocks):
                was_below = jnp.where(block > jm, 0, 1)
                lu[was_below, block * B : (block + 1) * B, last] = done[i * B : (i + 1) * B]

        def begin(blocks):
            known = jnp.concatenate(
                [lu[jnp.where(b > j, 0, 1), b * B : (b + 1) * B, :] for b in blocks], axis=0
            )
            t = dot(known, row_j)
            for i, block in enumerate(blocks):
                start = jnp.where(block > j, block_rows(j, block).astype(F32), 0.0)
                start = jnp.where(block == j, eye, start)
                tcol[block * B : (block + 1) * B, :] = (
                    start - t[i * B : (i + 1) * B]
                ).astype(BF16)

        def aside(p):
            if p in (3, 7, 11):
                arrive(j, (p + 1) // 4)
            if p == 3:
                row_next = lu[0, after, :]
                quad[...] = dot(row_next, row_next)
            for at, (do, blocks) in ASIDES:
                if at == p:
                    (finish if do == "finish" else begin)(blocks)

        factor([diagonal[8 * i : 8 * i + 8, :] for i in range(16)], w_ref, aside)
        new = dot(tcol[after, :], w_ref[...]).astype(BF16)
        quad[...] += dot(new, new)
        lu[0, after, now] = new
        return carry

    lax.fori_loop(0, NB, step, 0)
    for i in range(4):
        part = slice(i * 256, (i + 1) * 256)
        lu[1, part, N - B : N] = dot(tcol[part, :], w_ref[...]).astype(BF16)

    for way in range(2):
        p_copy(3, way).wait_recv()
    for i in range(8):
        if i == 2:
            s5_on()
        part = slice(i * B, (i + 1) * B)
        mine = jnp.concatenate([rows[c, part, :] for c in range(NB)], axis=1)
        for c in range(4):
            cols = slice(c * 256, (c + 1) * 256)
            deep = (c + 1) * 256
            fac[part, cols] = dot(mine[:, :deep], lu[1, :deep, cols], NN).astype(BF16)
        own_out[part, :] = fac[part, pl.ds(pl.multiple_of(z * B, B), B)]

    s6_copy().wait_recv()
    raw = jnp.concatenate(
        [jnp.concatenate([pick[i, c] for i in range(8)], axis=0) for c in range(NB)], axis=1
    )
    for c in range(4):
        cols = slice(c * 256, (c + 1) * 256)
        deep = (c + 1) * 256
        low_w[:, cols] = dot(raw[:, :deep], lu[1, :deep, cols], NN).astype(BF16)
    for i in range(8):
        part = slice(i * B, (i + 1) * B)
        update = dot(fac[part, :], low_w[...])
        left = slab[part, :].astype(F32) - update
        for c in range(2):
            cols = slice(c * B, (c + 1) * B)
            slab_out[part, cols] = (left[:, cols] * pattern[c, i].astype(F32)).astype(BF16)

    for g in range(4):
        for d in others:
            y_copy(g, d).wait_send()
        for d in range(1, 4):
            x_copy(g, d).wait_send()
        k_copy(g).wait_send()
    for hop in range(4):
        for way in range(2):
            p_copy(hop, way).wait_send()
    s0_copy().wait_send()
    for d in range(1, 4):
        s1_copy(d).wait_send()
    for d in others:
        c_copy(d).wait_send()
        s2_copy(d).wait_send()
        s5_copy(d).wait_send()

        @pl.when(z == q)
        def _():
            s4_copy(d).wait_send()

    s6_copy().wait_send()

    @pl.when(z != q)
    def _():
        s3_copy(z).wait_send()


def shards(pivot, panel, slab, pattern, col_source):
    vmem = pl.BlockSpec(memory_space=pltpu.VMEM)
    smem = pl.BlockSpec(memory_space=pltpu.SMEM)
    dma = pltpu.SemaphoreType.DMA
    return pl.pallas_call(
        kernel,
        out_shape=[
            jax.ShapeDtypeStruct((N, B), BF16),
            jax.ShapeDtypeStruct((N, 2 * B), BF16),
        ],
        in_specs=[vmem, vmem, vmem, smem, smem],
        out_specs=[vmem, vmem],
        scratch_shapes=[
            pltpu.VMEM((8, 4, 8, 2, 16, B), BF16),
            pltpu.VMEM((8, 8, B), I32),
            pltpu.VMEM((4, 2, 2 * B, B), BF16),
            pltpu.VMEM((4, 2 * B, B), BF16),
            pltpu.VMEM((4, 2 * B, B), BF16),
            pltpu.VMEM((4, 2 * B, B), BF16),
            pltpu.VMEM((8, 2 * B, B), BF16),
            pltpu.VMEM((9, 32, B), BF16),
            pltpu.VMEM((8, 32, B), BF16),
            pltpu.VMEM((8, 8, 32, B), BF16),
            pltpu.VMEM((8, N, B), BF16),
            pltpu.VMEM((2, N, N), BF16),
            pltpu.VMEM((N, B), BF16),
            pltpu.VMEM((B, B), F32),
            pltpu.VMEM((B, B), BF16),
            pltpu.VMEM((2 * B, N), BF16),
            pltpu.VMEM((N, N), BF16),
            dma((4, 8)), dma((4, 8)), dma((4, 4)), dma((4, 4)), dma((4,)), dma((4,)),
            dma((8,)), dma((8,)), dma((4, 2)), dma((4, 2)),
            dma((8,)), dma((8,)), dma((8,)), dma((8,)),
            dma, dma((8,)),
            dma((8,)), dma((8,)), dma((8,)), dma((8,)), dma, dma, dma, dma,
        ],
        compiler_params=pltpu.CompilerParams(
            collective_id=0, has_side_effects=True, vmem_limit_bytes=56 * 2**20
        ),
        cost_estimate=pl.CostEstimate(
            flops=5 * 10**9, bytes_accessed=2 * 2**20, transcendentals=0
        ),
    )(pivot, panel, slab, pattern.T, col_source)


def solution(mesh):
    return jax.shard_map(
        shards,
        mesh=mesh,
        in_specs=(P("row", None), P("row", "col"), P("row", "col"), P("row", "col"), P("col")),
        out_specs=(P("row", "col"), P("row", "col")),
        check_vma=False,
    )
```

```python
import jax
import jax.numpy as jnp
from jax import lax
from jax.experimental import pallas as pl
from jax.experimental.pallas import tpu as pltpu
from jax.sharding import PartitionSpec as P

F32, BF16, I32 = jnp.float32, jnp.bfloat16, jnp.int32
B = 128
NB = 8
N = 1024
MESH = pl.DeviceIdType.MESH
GROUPS = (slice(0, 1), slice(1, 2), slice(2, 4), slice(4, 8))
ASIDES = (
    (0, ("finish", (0, 1, 2, 3))),
    (1, ("finish", (4, 5, 6, 7))),
    (4, ("begin", (0,))),
    (5, ("begin", (1,))),
    (6, ("begin", (2,))),
    (7, ("begin", (3,))),
    (9, ("begin", (4,))),
    (10, ("begin", (5,))),
    (11, ("begin", (6,))),
    (12, ("begin", (7,))),
)
NT = (((1,), (1,)), ((), ()))
NN = (((1,), (0,)), ((), ()))


def dot(a, b, dims=NT):
    return lax.dot_general(a, b, dims, preferred_element_type=F32)


def lane_spread(x, lane):
    return jnp.broadcast_to(x[:, lane : lane + 1], (8, B))


def row_spread(x, row):
    return jnp.broadcast_to(x[row : row + 1, :], (8, B))


def factor(rows, w_ref, aside):
    lane = lax.broadcasted_iota(I32, (8, B), 1)
    sub = lax.broadcasted_iota(I32, (8, B), 0)
    rows = list(rows)
    before = None
    cols = [lane_spread(rows[0], j) for j in range(8)]
    for p in range(16):
        more = p < 15
        if more:
            left = [lane_spread(rows[p + 1], 8 * p + j) for j in range(8)]
            ahead = [lane_spread(rows[p + 1], 8 * p + 8 + j) for j in range(8)]
        inside = (lane >= 8 * p) & (lane < 8 * p + 8)
        unit = jnp.where(lane == 8 * p + sub, 1.0, 0.0).astype(F32)
        low = jnp.where(inside, unit, rows[p])
        full = low
        inverse = jnp.zeros((8, B), F32)
        for k in range(8):
            inv = 1.0 / row_spread(cols[k], k)
            mult = cols[k] * inv
            both = jnp.where(sub == k, 0.0, mult)
            below = jnp.where(sub > k, mult, 0.0)
            across = [None] * 8
            for j in range(k + 1, 8):
                across[j] = row_spread(cols[j], k)
                cols[j] = cols[j] - both * across[j]
            if more:
                mult = left[k] * inv
                for j in range(8):
                    ahead[j] = ahead[j] - mult * row_spread(left[k], j)
                for j in range(k + 1, 8):
                    left[j] = left[j] - mult * across[j]
            full = full - both * row_spread(full, k)
            low = low - below * row_spread(low, k)
            inverse = jnp.where(sub == k, inv, inverse)
        w = jnp.where(lane < 8 * p + 8, low * jnp.sqrt(inverse), 0.0)
        if p % 2 == 0:
            before = w
        else:
            w_ref[8 * p - 8 : 8 * p + 8, :] = jnp.concatenate([before, w], 0).astype(BF16)
        full = full * inverse
        spread = [row_spread(full, k) for k in range(8)]
        for q in range(p + 1, min(p + 3, 16)):
            v = rows[q]
            t = [lane_spread(v, 8 * p + k) * spread[k] for k in range(8)]
            total = ((t[0] + t[1]) + (t[2] + t[3])) + ((t[4] + t[5]) + (t[6] + t[7]))
            rows[q] = jnp.where(inside, 0.0, v) - total
        if p < 13:
            far = jnp.concatenate(rows[p + 3 :], 0) if p < 12 else rows[15]
            zero = jnp.zeros((8, B), F32)
            padded = jnp.concatenate([zero] * p + [full] + [zero] * (15 - p), 0).astype(BF16)
            total = dot(far.astype(BF16), padded, NN)
            for i, q in enumerate(range(p + 3, 16)):
                rows[q] = jnp.where(inside, 0.0, rows[q]) - total[8 * i : 8 * i + 8]
        if more:
            cols = ahead
        aside(p)


def kernel(
    pivot, panel, slab, pattern, col_source, own_out, slab_out,
    piv, cs, marked, part0, chip, part1, part2, part3, held, pick, rows, lu, tcol, quad, w_ref, low_w, fac,
    y_send, y_recv, x_send, x_recv, k_send, k_recv, c_send, c_recv, p_send, p_recv,
    s1_send, s1_recv, s2_send, s2_recv, s3_send, s3_recv, s4_send, s4_recv, s5_send, s5_recv, s6_send, s6_recv, s0_send, s0_recv,
):
    r = lax.axis_index("row")
    z = lax.axis_index("col")
    x, y, core = r // 16, (r // 2) % 8, r % 2
    q = x * 2 + core

    def at_y(d):
        return ((x * 8 + (y + d) % 8) * 2 + core, z)

    def at_q(d):
        o = (q + d) % 8
        return (((o // 2) * 8 + y) * 2 + o % 2, z)

    def at_x(d):
        return ((((x + d) % 4) * 8 + y) * 2 + core, z)

    def at_z(d):
        return (r, (z + d) % 8)

    def remote(src, dst, send, recv, device):
        return pltpu.make_async_remote_copy(
            src_ref=src, dst_ref=dst, send_sem=send, recv_sem=recv,
            device_id=device, device_id_type=MESH,
        )

    def y_copy(g, d):
        ref = piv.at[GROUPS[g], :, y, core] if g == 2 else piv.at[GROUPS[g], x, y, core]
        return remote(ref, ref, y_send.at[g, d], y_recv.at[g, d], at_y(d))

    def x_copy(g, d):
        ref = piv.at[GROUPS[g], x, y, core] if g == 2 else piv.at[GROUPS[g], x, :, core]
        return remote(ref, ref, x_send.at[g, d], x_recv.at[g, d], at_x(d))

    def k_copy(g):
        ref = piv.at[GROUPS[g], :, :, core]
        return remote(ref, ref, k_send.at[g], k_recv.at[g], (r + 1 - 2 * core, z))

    def c_copy(d):
        ref = cs.at[z]
        return remote(ref, ref, c_send.at[d], c_recv.at[d], at_z(d))

    def p_copy(hop, way):
        if way == 0:
            block, device = (z + 8 - hop) % 8, (r, (z + 1) % 8)
        else:
            block, device = (z + hop) % 8, (r, (z + 7) % 8)
        if hop == 0:
            src, dst = panel, rows.at[z]
        elif hop < 3:
            src = dst = rows.at[block]
        else:
            src = dst = rows.at[block, way * (N // 2) : (way + 1) * (N // 2)]
        return remote(src, dst, p_send.at[hop, way], p_recv.at[hop, way], device)

    def p_hop(hop):
        for way in range(2):
            if hop:
                p_copy(hop - 1, way).wait_recv()
        for way in range(2):
            p_copy(hop, way).start()

    def s0_copy():
        return remote(
            marked.at[:, 1 - core], part0, s0_send, s0_recv, (r + 1 - 2 * core, z)
        )

    def s1_copy(d):
        return remote(
            chip.at[(x + d) % 4], part1.at[d], s1_send.at[d], s1_recv.at[d], at_x(d)
        )

    def s2_copy(d):
        return remote(
            part2.at[0, pl.ds(((y + d) % 8) * 32, 32)], part2.at[d, 0:32],
            s2_send.at[d], s2_recv.at[d], at_y(d),
        )

    def s3_copy(source):
        return remote(
            part3.at[0], part3.at[1 + source], s3_send, s3_recv.at[source], (r, q)
        )

    def s4_copy(d):
        half = (q + d) % 2
        return remote(
            held.at[pl.ds(half * 4, 4)], pick.at[y, pl.ds(half * 4, 4)],
            s4_send.at[d], s4_recv.at[d], at_q(d),
        )

    def s5_copy(d):
        ref = pick.at[y, pl.ds(core * 4, 4)]
        return remote(ref, ref, s5_send.at[d], s5_recv.at[d], at_y(d))

    def s6_copy():
        ref = pick.at[:, pl.ds(core * 4, 4)]
        return remote(ref, ref, s6_send, s6_recv, (r + 1 - 2 * core, z))

    others = range(1, 8)

    barrier = pltpu.get_barrier_semaphore()
    for d in others:
        for device in (at_y(d), at_q(d), at_z(d)):
            pl.semaphore_signal(barrier, inc=1, device_id=device, device_id_type=MESH)

    for c in range(NB):
        piv[c, x, y, core] = pivot[:, c * B : (c + 1) * B].astype(BF16)
    sub = lax.broadcasted_iota(I32, (8, B), 0)
    cs[z] = jnp.where(sub == 0, col_source[0], col_source[1])

    pl.semaphore_wait(barrier, 21)
    for d in others:
        y_copy(0, d).start()
    for d in others:
        c_copy(d).start()
    for d in range(1, 4):
        x_copy(2, d).start()
    for g in (1, 3):
        for d in others:
            y_copy(g, d).start()
    p_hop(0)
    rows[z] = panel[...]
    lu[...] = jnp.zeros_like(lu)
    quad[...] = jnp.zeros_like(quad)
    tcol[...] = jnp.zeros_like(tcol)
    w_ref[...] = jnp.zeros_like(w_ref)
    for d in others:
        y_copy(0, d).wait_recv()
    for d in range(1, 4):
        x_copy(0, d).start()

    for d in others:
        c_copy(d).wait_recv()

    def mark(pair, carry):
        for t in range(2):
            wanted = cs[pair, t : t + 1, :]
            total = jnp.zeros((B, B), F32)
            for s in range(8):
                here = panel[s * B : (s + 1) * B, :].astype(F32)
                total = jnp.where(wanted == r * 8 + s, here, total)
            marked[pair // 2, pair % 2, t * B : (t + 1) * B, :] = total.astype(BF16)
        return carry

    lax.fori_loop(0, 8, mark, 0)
    s0_copy().start()
    for d in others:
        y_copy(1, d).wait_recv()
    for d in range(1, 4):
        x_copy(1, d).start()
    for d in range(1, 4):
        x_copy(2, d).wait_recv()
    for d in others:
        y_copy(2, d).start()
    for d in range(1, 4):
        x_copy(0, d).wait_recv()
    k_copy(0).start()
    s0_copy().wait_recv()
    for i in range(4):
        chip[i] = marked[i, core] + part0[i]
    for d in range(1, 4):
        s1_copy(d).start()
    for d in range(1, 4):
        x_copy(1, d).wait_recv()
    k_copy(1).start()

    def block_rows(column, block):
        return piv[column, block // 2, pl.ds((block % 2) * 4, 4)].reshape(B, B)

    def s1_on():
        total = chip[x].astype(F32)
        for d in range(1, 4):
            s1_copy(d).wait_recv()
        for d in range(1, 4):
            total += part1[d].astype(F32)
        part2[0] = total.astype(BF16)
        for d in others:
            s2_copy(d).start()

    def s2_on():
        for d in others:
            s2_copy(d).wait_recv()
        total = part2[0, pl.ds(y * 32, 32), :].astype(F32)
        for d in others:
            total += part2[d, 0:32, :].astype(F32)
        part3[0] = total.astype(BF16)

        @pl.when(z != q)
        def _():
            s3_copy(z).start()

    def s3_on():
        @pl.when(z == q)
        def _():
            for s in range(8):
                @pl.when(z != s)
                def _():
                    s3_copy(s).wait_recv()
                    held[s] = part3[1 + s]
            held[z] = part3[0]
            pick[y, pl.ds(core * 4, 4)] = held[pl.ds(core * 4, 4)]
            for d in others:
                s4_copy(d).start()

    def s4_on():
        for d in others:
            @pl.when((q + 8 - d) % 8 == z)
            def _():
                s4_copy(d).wait_recv()
        for d in others:
            s5_copy(d).start()

    def s5_on():
        for d in others:
            s5_copy(d).wait_recv()
        s6_copy().start()

    def y2_on():
        for d in others:
            y_copy(2, d).wait_recv()
        k_copy(2).start()

    def y3_on():
        for d in others:
            y_copy(3, d).wait_recv()
        for d in range(1, 4):
            x_copy(3, d).start()

    def x3_on():
        for d in range(1, 4):
            x_copy(3, d).wait_recv()
        k_copy(3).start()

    plan = {
        0: [lambda: k_copy(0).wait_recv()],
        1: [lambda: p_hop(1)],
        2: [y3_on],
        4: [lambda: k_copy(1).wait_recv()],
        5: [y2_on],
        6: [s1_on],
        8: [lambda: k_copy(2).wait_recv()],
        12: [s2_on],
        13: [x3_on, lambda: p_hop(2)],
        16: [lambda: k_copy(3).wait_recv(), s3_on],
        22: [s4_on],
        24: [lambda: p_hop(3)],
    }

    def arrive(j, quarter):
        for at, parts in plan.items():
            if at % 4 == quarter:
                @pl.when(j == at // 4)
                def _():
                    for part in parts:
                        part()

    def step(j, carry):
        arrive(j, 0)
        jm = jnp.maximum(j - 1, 0)
        jn = jnp.minimum(j + 1, NB - 1)
        now = pl.ds(pl.multiple_of(j * B, B), B)
        last = pl.ds(pl.multiple_of(jm * B, B), B)
        after = pl.ds(pl.multiple_of(jn * B, B), B)
        w_old = w_ref[...]
        row_j = lu[0, now, :]
        diagonal = block_rows(j, j).astype(F32) - quad[...]
        lu[0, after, last] = dot(tcol[after, :], w_old).astype(BF16)
        eye = jnp.where(
            lax.broadcasted_iota(I32, (B, B), 0) == lax.broadcasted_iota(I32, (B, B), 1), 1.0, 0.0
        ).astype(F32)

        def finish(blocks):
            done = dot(tcol[blocks[0] * B : (blocks[-1] + 1) * B, :], w_old).astype(BF16)
            for i, block in enumerate(blocks):
                was_below = jnp.where(block > jm, 0, 1)
                lu[was_below, block * B : (block + 1) * B, last] = done[i * B : (i + 1) * B]

        def begin(blocks):
            known = jnp.concatenate(
                [lu[jnp.where(b > j, 0, 1), b * B : (b + 1) * B, :] for b in blocks], axis=0
            )
            t = dot(known, row_j)
            for i, block in enumerate(blocks):
                start = jnp.where(block > j, block_rows(j, block).astype(F32), 0.0)
                start = jnp.where(block == j, eye, start)
                tcol[block * B : (block + 1) * B, :] = (
                    start - t[i * B : (i + 1) * B]
                ).astype(BF16)

        def aside(p):
            if p in (3, 7, 11):
                arrive(j, (p + 1) // 4)
            if p == 3:
                row_next = lu[0, after, :]
                quad[...] = dot(row_next, row_next)
            for at, (do, blocks) in ASIDES:
                if at == p:
                    (finish if do == "finish" else begin)(blocks)

        factor([diagonal[8 * i : 8 * i + 8, :] for i in range(16)], w_ref, aside)
        new = dot(tcol[after, :], w_ref[...]).astype(BF16)
        quad[...] += dot(new, new)
        lu[0, after, now] = new
        return carry

    lax.fori_loop(0, NB, step, 0)
    for i in range(4):
        part = slice(i * 256, (i + 1) * 256)
        lu[1, part, N - B : N] = dot(tcol[part, :], w_ref[...]).astype(BF16)

    for way in range(2):
        p_copy(3, way).wait_recv()
    for i in range(4):
        if i == 1:
            s5_on()
        part = slice(i * 256, (i + 1) * 256)
        for c in range(4):
            cols = slice(c * 256, (c + 1) * 256)
            deep = 2 * (c + 1)
            mine = jnp.concatenate([rows[k, part, :] for k in range(deep)], axis=1)
            fac[part, cols] = dot(mine, lu[1, : deep * B, cols], NN).astype(BF16)
        own_out[part, :] = fac[part, pl.ds(pl.multiple_of(z * B, B), B)]

    s6_copy().wait_recv()
    raw = jnp.concatenate(
        [jnp.concatenate([pick[i, c] for i in range(8)], axis=0) for c in range(NB)], axis=1
    )
    for c in range(4):
        cols = slice(c * 256, (c + 1) * 256)
        deep = (c + 1) * 256
        low_w[:, cols] = dot(raw[:, :deep], lu[1, :deep, cols], NN).astype(BF16)
    for i in range(2):
        part = slice(i * 512, (i + 1) * 512)
        update = dot(fac[part, :], low_w[...])
        for k in range(4):
            for c in range(2):
                cols = slice(c * B, (c + 1) * B)
                here = slice(i * 512 + k * B, i * 512 + (k + 1) * B)
                left = slab[here, cols].astype(F32) - update[k * B : (k + 1) * B, cols]
                slab_out[here, cols] = (left * pattern[c, i * 4 + k].astype(F32)).astype(BF16)

    for g in range(4):
        for d in others:
            y_copy(g, d).wait_send()
        for d in range(1, 4):
            x_copy(g, d).wait_send()
        k_copy(g).wait_send()
    for hop in range(4):
        for way in range(2):
            p_copy(hop, way).wait_send()
    s0_copy().wait_send()
    for d in range(1, 4):
        s1_copy(d).wait_send()
    for d in others:
        c_copy(d).wait_send()
        s2_copy(d).wait_send()
        s5_copy(d).wait_send()

        @pl.when(z == q)
        def _():
            s4_copy(d).wait_send()

    s6_copy().wait_send()

    @pl.when(z != q)
    def _():
        s3_copy(z).wait_send()


def shards(pivot, panel, slab, pattern, col_source):
    vmem = pl.BlockSpec(memory_space=pltpu.VMEM)
    smem = pl.BlockSpec(memory_space=pltpu.SMEM)
    dma = pltpu.SemaphoreType.DMA
    return pl.pallas_call(
        kernel,
        out_shape=[
            jax.ShapeDtypeStruct((N, B), BF16),
            jax.ShapeDtypeStruct((N, 2 * B), BF16),
        ],
        in_specs=[vmem, vmem, vmem, smem, smem],
        out_specs=[vmem, vmem],
        scratch_shapes=[
            pltpu.VMEM((8, 4, 8, 2, 16, B), BF16),
            pltpu.VMEM((8, 8, B), I32),
            pltpu.VMEM((4, 2, 2 * B, B), BF16),
            pltpu.VMEM((4, 2 * B, B), BF16),
            pltpu.VMEM((4, 2 * B, B), BF16),
            pltpu.VMEM((4, 2 * B, B), BF16),
            pltpu.VMEM((8, 2 * B, B), BF16),
            pltpu.VMEM((9, 32, B), BF16),
            pltpu.VMEM((8, 32, B), BF16),
            pltpu.VMEM((8, 8, 32, B), BF16),
            pltpu.VMEM((8, N, B), BF16),
            pltpu.VMEM((2, N, N), BF16),
            pltpu.VMEM((N, B), BF16),
            pltpu.VMEM((B, B), F32),
            pltpu.VMEM((B, B), BF16),
            pltpu.VMEM((2 * B, N), BF16),
            pltpu.VMEM((N, N), BF16),
            dma((4, 8)), dma((4, 8)), dma((4, 4)), dma((4, 4)), dma((4,)), dma((4,)),
            dma((8,)), dma((8,)), dma((4, 2)), dma((4, 2)),
            dma((8,)), dma((8,)), dma((8,)), dma((8,)),
            dma, dma((8,)),
            dma((8,)), dma((8,)), dma((8,)), dma((8,)), dma, dma, dma, dma,
        ],
        compiler_params=pltpu.CompilerParams(
            collective_id=0, has_side_effects=True, vmem_limit_bytes=56 * 2**20
        ),
        cost_estimate=pl.CostEstimate(
            flops=5 * 10**9, bytes_accessed=2 * 2**20, transcendentals=0
        ),
    )(pivot, panel, slab, pattern.T, col_source)


def solution(mesh):
    return jax.shard_map(
        shards,
        mesh=mesh,
        in_specs=(P("row", None), P("row", "col"), P("row", "col"), P("row", "col"), P("col")),
        out_specs=(P("row", "col"), P("row", "col")),
        check_vma=False,
    )
```

```python
import jax
import jax.numpy as jnp
from jax import lax
from jax.experimental import pallas as pl
from jax.experimental.pallas import tpu as pltpu
from jax.sharding import PartitionSpec as P

F32, BF16, I32 = jnp.float32, jnp.bfloat16, jnp.int32
B = 128
NB = 8
N = 1024
MESH = pl.DeviceIdType.MESH
GROUPS = (slice(0, 1), slice(1, 2), slice(2, 4), slice(4, 8))
ASIDES = (
    (0, ("finish", (0, 1, 2, 3))),
    (1, ("finish", (4, 5, 6, 7))),
    (4, ("begin", (0,))),
    (5, ("begin", (1,))),
    (6, ("begin", (2,))),
    (7, ("begin", (3,))),
    (9, ("begin", (4,))),
    (10, ("begin", (5,))),
    (11, ("begin", (6,))),
    (12, ("begin", (7,))),
)
NT = (((1,), (1,)), ((), ()))
NN = (((1,), (0,)), ((), ()))


def dot(a, b, dims=NT):
    return lax.dot_general(a, b, dims, preferred_element_type=F32)


def lane_spread(x, lane):
    return jnp.broadcast_to(x[:, lane : lane + 1], (8, B))


def row_spread(x, row):
    return jnp.broadcast_to(x[row : row + 1, :], (8, B))


def factor(rows, w_ref, aside):
    lane = lax.broadcasted_iota(I32, (8, B), 1)
    sub = lax.broadcasted_iota(I32, (8, B), 0)
    rows = list(rows)
    before = None
    cols = [lane_spread(rows[0], j) for j in range(8)]
    for p in range(16):
        more = p < 15
        if more:
            left = [lane_spread(rows[p + 1], 8 * p + j) for j in range(8)]
            ahead = [lane_spread(rows[p + 1], 8 * p + 8 + j) for j in range(8)]
        inside = (lane >= 8 * p) & (lane < 8 * p + 8)
        unit = jnp.where(lane == 8 * p + sub, 1.0, 0.0).astype(F32)
        low = jnp.where(inside, unit, rows[p])
        full = low
        inverse = jnp.zeros((8, B), F32)
        for k in range(8):
            inv = 1.0 / row_spread(cols[k], k)
            mult = cols[k] * inv
            both = jnp.where(sub == k, 0.0, mult)
            below = jnp.where(sub > k, mult, 0.0)
            across = [None] * 8
            for j in range(k + 1, 8):
                across[j] = row_spread(cols[j], k)
                cols[j] = cols[j] - both * across[j]
            if more:
                mult = left[k] * inv
                for j in range(8):
                    ahead[j] = ahead[j] - mult * row_spread(left[k], j)
                for j in range(k + 1, 8):
                    left[j] = left[j] - mult * across[j]
            full = full - both * row_spread(full, k)
            low = low - below * row_spread(low, k)
            inverse = jnp.where(sub == k, inv, inverse)
        w = jnp.where(lane < 8 * p + 8, low * jnp.sqrt(inverse), 0.0)
        if p % 2 == 0:
            before = w
        else:
            w_ref[8 * p - 8 : 8 * p + 8, :] = jnp.concatenate([before, w], 0).astype(BF16)
        full = full * inverse
        spread = [row_spread(full, k) for k in range(8)]
        for q in range(p + 1, min(p + 3, 16)):
            v = rows[q]
            t = [lane_spread(v, 8 * p + k) * spread[k] for k in range(8)]
            total = ((t[0] + t[1]) + (t[2] + t[3])) + ((t[4] + t[5]) + (t[6] + t[7]))
            rows[q] = jnp.where(inside, 0.0, v) - total
        if p < 13:
            far = jnp.concatenate(rows[p + 3 :], 0) if p < 12 else rows[15]
            zero = jnp.zeros((8, B), F32)
            padded = jnp.concatenate([zero] * p + [full] + [zero] * (15 - p), 0).astype(BF16)
            total = dot(far.astype(BF16), padded, NN)
            for i, q in enumerate(range(p + 3, 16)):
                rows[q] = jnp.where(inside, 0.0, rows[q]) - total[8 * i : 8 * i + 8]
        if more:
            cols = ahead
        aside(p)


def kernel(
    pivot, panel, slab, pattern, col_source, own_out, slab_out,
    piv, cs, marked, part0, chip, part1, part2, part3, held, pick, rows, lu, tcol, quad, w_ref, low_w, fac,
    y_send, y_recv, x_send, x_recv, k_send, k_recv, c_send, c_recv, p_send, p_recv,
    s1_send, s1_recv, s2_send, s2_recv, s3_send, s3_recv, s4_send, s4_recv, s5_send, s5_recv, s6_send, s6_recv, s0_send, s0_recv,
):
    r = lax.axis_index("row")
    z = lax.axis_index("col")
    x, y, core = r // 16, (r // 2) % 8, r % 2
    q = x * 2 + core

    def at_y(d):
        return ((x * 8 + (y + d) % 8) * 2 + core, z)

    def at_q(d):
        o = (q + d) % 8
        return (((o // 2) * 8 + y) * 2 + o % 2, z)

    def at_x(d):
        return ((((x + d) % 4) * 8 + y) * 2 + core, z)

    def at_z(d):
        return (r, (z + d) % 8)

    def remote(src, dst, send, recv, device):
        return pltpu.make_async_remote_copy(
            src_ref=src, dst_ref=dst, send_sem=send, recv_sem=recv,
            device_id=device, device_id_type=MESH,
        )

    def y_copy(g, d):
        ref = piv.at[GROUPS[g], :, y, core] if g == 2 else piv.at[GROUPS[g], x, y, core]
        return remote(ref, ref, y_send.at[g, d], y_recv.at[g, d], at_y(d))

    def x_copy(g, d):
        ref = piv.at[GROUPS[g], x, y, core] if g == 2 else piv.at[GROUPS[g], x, :, core]
        return remote(ref, ref, x_send.at[g, d], x_recv.at[g, d], at_x(d))

    def k_copy(g):
        ref = piv.at[GROUPS[g], :, :, core]
        return remote(ref, ref, k_send.at[g], k_recv.at[g], (r + 1 - 2 * core, z))

    def c_copy(d):
        ref = cs.at[z]
        return remote(ref, ref, c_send.at[d], c_recv.at[d], at_z(d))

    def p_copy(hop, way):
        if way == 0:
            block, device = (z + 8 - hop) % 8, (r, (z + 1) % 8)
        else:
            block, device = (z + hop) % 8, (r, (z + 7) % 8)
        if hop == 0:
            src, dst = panel, rows.at[z]
        elif hop < 3:
            src = dst = rows.at[block]
        else:
            src = dst = rows.at[block, way * (N // 2) : (way + 1) * (N // 2)]
        return remote(src, dst, p_send.at[hop, way], p_recv.at[hop, way], device)

    def p_hop(hop):
        for way in range(2):
            if hop:
                p_copy(hop - 1, way).wait_recv()
        for way in range(2):
            p_copy(hop, way).start()

    def s0_copy():
        return remote(
            marked.at[:, 1 - core], part0, s0_send, s0_recv, (r + 1 - 2 * core, z)
        )

    def s1_copy(d):
        return remote(
            chip.at[(x + d) % 4], part1.at[d], s1_send.at[d], s1_recv.at[d], at_x(d)
        )

    def s2_copy(d):
        return remote(
            part2.at[0, pl.ds(((y + d) % 8) * 32, 32)], part2.at[d, 0:32],
            s2_send.at[d], s2_recv.at[d], at_y(d),
        )

    def s3_copy(source):
        return remote(
            part3.at[0], part3.at[1 + source], s3_send, s3_recv.at[source], (r, q)
        )

    def s4_copy(d):
        half = (q + d) % 2
        return remote(
            held.at[pl.ds(half * 4, 4)], pick.at[y, pl.ds(half * 4, 4)],
            s4_send.at[d], s4_recv.at[d], at_q(d),
        )

    def s5_copy(d):
        ref = pick.at[y, pl.ds(core * 4, 4)]
        return remote(ref, ref, s5_send.at[d], s5_recv.at[d], at_y(d))

    def s6_copy():
        ref = pick.at[:, pl.ds(core * 4, 4)]
        return remote(ref, ref, s6_send, s6_recv, (r + 1 - 2 * core, z))

    others = range(1, 8)

    barrier = pltpu.get_barrier_semaphore()
    for d in others:
        for device in (at_y(d), at_q(d), at_z(d)):
            pl.semaphore_signal(barrier, inc=1, device_id=device, device_id_type=MESH)

    for c in range(NB):
        piv[c, x, y, core] = pivot[:, c * B : (c + 1) * B].astype(BF16)
    sub = lax.broadcasted_iota(I32, (8, B), 0)
    cs[z] = jnp.where(sub == 0, col_source[0], col_source[1])

    pl.semaphore_wait(barrier, 21)
    for d in others:
        y_copy(0, d).start()
    for d in others:
        c_copy(d).start()
    for d in range(1, 4):
        x_copy(2, d).start()
    for g in (1, 3):
        for d in others:
            y_copy(g, d).start()
    p_hop(0)
    rows[z] = panel[...]
    lu[...] = jnp.zeros_like(lu)
    quad[...] = jnp.zeros_like(quad)
    tcol[...] = jnp.zeros_like(tcol)
    w_ref[...] = jnp.zeros_like(w_ref)
    for d in others:
        y_copy(0, d).wait_recv()
    for d in range(1, 4):
        x_copy(0, d).start()

    for d in others:
        c_copy(d).wait_recv()

    def mark(pair, carry):
        for t in range(2):
            wanted = cs[pair, t : t + 1, :]
            total = jnp.zeros((B, B), F32)
            for s in range(8):
                here = panel[s * B : (s + 1) * B, :].astype(F32)
                total = jnp.where(wanted == r * 8 + s, here, total)
            marked[pair // 2, pair % 2, t * B : (t + 1) * B, :] = total.astype(BF16)
        return carry

    lax.fori_loop(0, 8, mark, 0)
    s0_copy().start()
    for d in others:
        y_copy(1, d).wait_recv()
    for d in range(1, 4):
        x_copy(1, d).start()
    for d in range(1, 4):
        x_copy(2, d).wait_recv()
    for d in others:
        y_copy(2, d).start()
    for d in range(1, 4):
        x_copy(0, d).wait_recv()
    k_copy(0).start()
    s0_copy().wait_recv()
    for i in range(4):
        chip[i] = marked[i, core] + part0[i]
    for d in range(1, 4):
        s1_copy(d).start()
    for d in range(1, 4):
        x_copy(1, d).wait_recv()
    k_copy(1).start()

    def block_rows(column, block):
        return piv[column, block // 2, pl.ds((block % 2) * 4, 4)].reshape(B, B)

    def s1_on():
        total = chip[x].astype(F32)
        for d in range(1, 4):
            s1_copy(d).wait_recv()
        for d in range(1, 4):
            total += part1[d].astype(F32)
        part2[0] = total.astype(BF16)
        for d in others:
            s2_copy(d).start()

    def s2_on():
        for d in others:
            s2_copy(d).wait_recv()
        total = part2[0, pl.ds(y * 32, 32), :].astype(F32)
        for d in others:
            total += part2[d, 0:32, :].astype(F32)
        part3[0] = total.astype(BF16)

        @pl.when(z != q)
        def _():
            s3_copy(z).start()

    def s3_on():
        @pl.when(z == q)
        def _():
            for s in range(8):
                @pl.when(z != s)
                def _():
                    s3_copy(s).wait_recv()
                    held[s] = part3[1 + s]
            held[z] = part3[0]
            pick[y, pl.ds(core * 4, 4)] = held[pl.ds(core * 4, 4)]
            for d in others:
                s4_copy(d).start()

    def s4_on():
        for d in others:
            @pl.when((q + 8 - d) % 8 == z)
            def _():
                s4_copy(d).wait_recv()
        for d in others:
            s5_copy(d).start()

    def s5_on():
        for d in others:
            s5_copy(d).wait_recv()
        s6_copy().start()

    def y2_on():
        for d in others:
            y_copy(2, d).wait_recv()
        k_copy(2).start()

    def y3_on():
        for d in others:
            y_copy(3, d).wait_recv()
        for d in range(1, 4):
            x_copy(3, d).start()

    def x3_on():
        for d in range(1, 4):
            x_copy(3, d).wait_recv()
        k_copy(3).start()

    plan = {
        0: [lambda: k_copy(0).wait_recv()],
        1: [lambda: p_hop(1)],
        3: [y3_on],
        4: [lambda: k_copy(1).wait_recv()],
        6: [y2_on],
        7: [s1_on],
        8: [lambda: k_copy(2).wait_recv()],
        13: [s2_on],
        14: [x3_on, lambda: p_hop(2)],
        16: [lambda: k_copy(3).wait_recv()],
        17: [s3_on],
        23: [s4_on],
        24: [lambda: p_hop(3)],
    }

    def arrive(j, quarter):
        for at, parts in plan.items():
            if at % 4 == quarter:
                @pl.when(j == at // 4)
                def _():
                    for part in parts:
                        part()

    def step(j, carry):
        arrive(j, 0)
        jm = jnp.maximum(j - 1, 0)
        jn = jnp.minimum(j + 1, NB - 1)
        now = pl.ds(pl.multiple_of(j * B, B), B)
        last = pl.ds(pl.multiple_of(jm * B, B), B)
        after = pl.ds(pl.multiple_of(jn * B, B), B)
        w_old = w_ref[...]
        row_j = lu[0, now, :]
        diagonal = block_rows(j, j).astype(F32) - quad[...]
        lu[0, after, last] = dot(tcol[after, :], w_old).astype(BF16)
        eye = jnp.where(
            lax.broadcasted_iota(I32, (B, B), 0) == lax.broadcasted_iota(I32, (B, B), 1), 1.0, 0.0
        ).astype(F32)

        def finish(blocks):
            done = dot(tcol[blocks[0] * B : (blocks[-1] + 1) * B, :], w_old).astype(BF16)
            for i, block in enumerate(blocks):
                was_below = jnp.where(block > jm, 0, 1)
                lu[was_below, block * B : (block + 1) * B, last] = done[i * B : (i + 1) * B]

        def begin(blocks):
            known = jnp.concatenate(
                [lu[jnp.where(b > j, 0, 1), b * B : (b + 1) * B, :] for b in blocks], axis=0
            )
            t = dot(known, row_j)
            for i, block in enumerate(blocks):
                start = jnp.where(block > j, block_rows(j, block).astype(F32), 0.0)
                start = jnp.where(block == j, eye, start)
                tcol[block * B : (block + 1) * B, :] = (
                    start - t[i * B : (i + 1) * B]
                ).astype(BF16)

        def aside(p):
            if p in (3, 7, 11):
                arrive(j, (p + 1) // 4)
            if p == 3:
                row_next = lu[0, after, :]
                quad[...] = dot(row_next, row_next)
            for at, (do, blocks) in ASIDES:
                if at == p:
                    (finish if do == "finish" else begin)(blocks)

        factor([diagonal[8 * i : 8 * i + 8, :] for i in range(16)], w_ref, aside)
        new = dot(tcol[after, :], w_ref[...]).astype(BF16)
        quad[...] += dot(new, new)
        lu[0, after, now] = new
        return carry

    lax.fori_loop(0, NB, step, 0)
    for i in range(4):
        part = slice(i * 256, (i + 1) * 256)
        lu[1, part, N - B : N] = dot(tcol[part, :], w_ref[...]).astype(BF16)

    for way in range(2):
        p_copy(3, way).wait_recv()
    for i in range(4):
        if i == 2:
            s5_on()
        part = slice(i * 256, (i + 1) * 256)
        for c in range(4):
            cols = slice(c * 256, (c + 1) * 256)
            deep = 2 * (c + 1)
            mine = jnp.concatenate([rows[k, part, :] for k in range(deep)], axis=1)
            fac[part, cols] = dot(mine, lu[1, : deep * B, cols], NN).astype(BF16)
        own_out[part, :] = fac[part, pl.ds(pl.multiple_of(z * B, B), B)]

    s6_copy().wait_recv()
    raw = jnp.concatenate(
        [jnp.concatenate([pick[i, c] for i in range(8)], axis=0) for c in range(NB)], axis=1
    )
    for c in range(4):
        cols = slice(c * 256, (c + 1) * 256)
        deep = (c + 1) * 256
        low_w[:, cols] = dot(raw[:, :deep], lu[1, :deep, cols], NN).astype(BF16)
    for i in range(2):
        part = slice(i * 512, (i + 1) * 512)
        update = dot(fac[part, :], low_w[...])
        for k in range(4):
            for c in range(2):
                cols = slice(c * B, (c + 1) * B)
                here = slice(i * 512 + k * B, i * 512 + (k + 1) * B)
                left = slab[here, cols].astype(F32) - update[k * B : (k + 1) * B, cols]
                slab_out[here, cols] = (left * pattern[c, i * 4 + k].astype(F32)).astype(BF16)

    for g in range(4):
        for d in others:
            y_copy(g, d).wait_send()
        for d in range(1, 4):
            x_copy(g, d).wait_send()
        k_copy(g).wait_send()
    for hop in range(4):
        for way in range(2):
            p_copy(hop, way).wait_send()
    s0_copy().wait_send()
    for d in range(1, 4):
        s1_copy(d).wait_send()
    for d in others:
        c_copy(d).wait_send()
        s2_copy(d).wait_send()
        s5_copy(d).wait_send()

        @pl.when(z == q)
        def _():
            s4_copy(d).wait_send()

    s6_copy().wait_send()

    @pl.when(z != q)
    def _():
        s3_copy(z).wait_send()


def shards(pivot, panel, slab, pattern, col_source):
    vmem = pl.BlockSpec(memory_space=pltpu.VMEM)
    smem = pl.BlockSpec(memory_space=pltpu.SMEM)
    dma = pltpu.SemaphoreType.DMA
    return pl.pallas_call(
        kernel,
        out_shape=[
            jax.ShapeDtypeStruct((N, B), BF16),
            jax.ShapeDtypeStruct((N, 2 * B), BF16),
        ],
        in_specs=[vmem, vmem, vmem, smem, smem],
        out_specs=[vmem, vmem],
        scratch_shapes=[
            pltpu.VMEM((8, 4, 8, 2, 16, B), BF16),
            pltpu.VMEM((8, 8, B), I32),
            pltpu.VMEM((4, 2, 2 * B, B), BF16),
            pltpu.VMEM((4, 2 * B, B), BF16),
            pltpu.VMEM((4, 2 * B, B), BF16),
            pltpu.VMEM((4, 2 * B, B), BF16),
            pltpu.VMEM((8, 2 * B, B), BF16),
            pltpu.VMEM((9, 32, B), BF16),
            pltpu.VMEM((8, 32, B), BF16),
            pltpu.VMEM((8, 8, 32, B), BF16),
            pltpu.VMEM((8, N, B), BF16),
            pltpu.VMEM((2, N, N), BF16),
            pltpu.VMEM((N, B), BF16),
            pltpu.VMEM((B, B), F32),
            pltpu.VMEM((B, B), BF16),
            pltpu.VMEM((2 * B, N), BF16),
            pltpu.VMEM((N, N), BF16),
            dma((4, 8)), dma((4, 8)), dma((4, 4)), dma((4, 4)), dma((4,)), dma((4,)),
            dma((8,)), dma((8,)), dma((4, 2)), dma((4, 2)),
            dma((8,)), dma((8,)), dma((8,)), dma((8,)),
            dma, dma((8,)),
            dma((8,)), dma((8,)), dma((8,)), dma((8,)), dma, dma, dma, dma,
        ],
        compiler_params=pltpu.CompilerParams(
            collective_id=0, has_side_effects=True, vmem_limit_bytes=56 * 2**20
        ),
        cost_estimate=pl.CostEstimate(
            flops=5 * 10**9, bytes_accessed=2 * 2**20, transcendentals=0
        ),
    )(pivot, panel, slab, pattern.T, col_source)


def solution(mesh):
    return jax.shard_map(
        shards,
        mesh=mesh,
        in_specs=(P("row", None), P("row", "col"), P("row", "col"), P("row", "col"), P("col")),
        out_specs=(P("row", "col"), P("row", "col")),
        check_vma=False,
    )
```
